32 devices in a mesh: tm: 8 (over z, y), band: 4 (over x, core).
Axes of the slice: x: 2, y: 2, z: 4, core: 2. Of those that a mesh axis runs over, the one named last changes fastest.
Arguments:
- queries: bfloat16 [16, 16, 16, 5120], P('tm', 'band'), may hold values from -118 to 118
- key_states: bfloat16 [16, 16, 16, 5120], P('tm', 'band'), may hold values from -4 to 4
- value_states: bfloat16 [16, 16, 16, 5120], P('tm', 'band'), may hold values from -5 to 5
- cotangent: bfloat16 [16, 16, 16, 5120], P('tm', 'band'), may hold values from -5 to 5
- frame_blocks: int32 [16], replicated, may hold values from 0 to 7, never falling along the last dimension, each value on 1 to 3 neighbouring positions
- tile_lists: int32 [8, 2, 2, 10], replicated, may hold values from 0 to 11, as said below
Outputs:
- attended: bfloat16 [16, 16, 16, 5120], P('tm', 'band')
- grad_queries: bfloat16 [16, 16, 16, 5120], P('tm', 'band')
- grad_keys: bfloat16 [16, 16, 16, 5120], P('tm', 'band')
- grad_values: bfloat16 [16, 16, 16, 5120], P('tm', 'band')
The draws below stay inside these ranges and needn't reach their ends.
Inputs may be any that keep to these rules, and one draw needn't show every extreme that they name: tile_lists[s, a, b] holds 10 distinct ids for tile a * 2 + b of slab s; id d * 4 + i names tile i of the slab d slabs earlier; the first id is always the tile itself.
All inputs are finite; a program needn't handle non-finite values.
Results may differ from the reference program's by a relative error of at most 0.011.
Values may be sent and summed in bfloat16 or wider, within the bound.
No kernel may reach another device: no remote copies, remote signals or barrier semaphores. Data moves between devices by JAX's collectives and lax.ppermute only.
A program may use at most 128 MiB of HBM per device.

```python
import math
import jax
import jax.numpy as jnp
import numpy as np
from jax import lax

HEAD_DIM = 128
TT = 2
TH = 8
TW = 8
NTH = 2
NTW = 2
K_NB = 10
D = 5120
H = 16
W = 16
TPS = 4
TILE = 128
NT = 16
BLOCKS = 8
N_TM = 8


def shared_keys(key):
    return jnp.clip(jax.random.normal(jax.random.fold_in(key, 11), (NT, H, W, D), jnp.float32), -4.0, 4.0)


def draw_key_states(key, part):
    base_rows = shared_keys(key)
    return base_rows.astype(jnp.bfloat16)


def draw_queries(key, part):
    key = jax.random.fold_in(key, 5)
    key_one = jax.random.fold_in(key, 0)
    result = jnp.clip(jax.random.normal(key_one, (NT, H, W, D), jnp.float32), -4.0, 4.0)
    return result.astype(jnp.bfloat16)


def draw_tile_lists(key, part):
    key = jax.random.fold_in(key, 7)
    row_count = N_TM * TPS
    row_keys = jax.random.split(key, row_count)
    own_tiles = jnp.tile(jnp.arange(TPS, dtype=jnp.int32), N_TM)

    def one_row(row_key, own_tile):
        shuffled = jax.random.permutation(row_key, 3 * TPS - 1).astype(jnp.int32)
        others = shuffled + (shuffled >= own_tile).astype(jnp.int32)
        return jnp.concatenate([own_tile[None], others[:K_NB - 1]])
    id_lists = jax.vmap(one_row)(row_keys, own_tiles)
    return id_lists.reshape(N_TM, NTH, NTW, K_NB).astype(jnp.int32)


def block_levels(key, dims, cuts, smallest, largest):
    factor_of, own = 1.0, jax.random.fold_in(key, 6)
    for axis_at, parts in cuts:
        draws = jnp.exp(jax.random.uniform(jax.random.fold_in(own, axis_at), (parts,), jnp.float32, smallest / len(cuts), largest / len(cuts)))
        factor_of = factor_of * jnp.repeat(draws, dims[axis_at] // parts).reshape([-1 if axis == axis_at else 1 for axis in range(len(dims))])
    return factor_of


def length_profile(count, total, limit, slope):
    portions = [(1 << 20) // math.isqrt(rank ** slope) + 1 for rank in range(2, count + 1)]
    surplus, counts = total - limit - (count - 1), [1] * (count - 1)
    while surplus > 0:
        candidates = [i for i in range(count - 1) if counts[i] < limit]
        whole, left = sum([portions[i] for i in candidates]), surplus
        for i in candidates:
            more = min(limit - counts[i], max(1, left * portions[i] // whole), surplus)
            counts[i] = counts[i] + more
            surplus = surplus - more
    return np.array([limit] + counts)


def uneven(rng, count, total, limit, lean):
    if count == 2:
        one = jax.random.randint(rng, (), max(1, total - limit), min(limit, total - 1) + 1)
        return jnp.stack([one, total - one])
    sizes = jnp.asarray(length_profile(count, total, limit, lean), jnp.int32)
    couples = (count - 1) // 2
    donor, taker = sizes[1:1 + 2 * couples:2], sizes[2:2 + 2 * couples:2]
    margin = jnp.minimum(donor - 1, limit - taker)
    passed = jax.random.randint(jax.random.fold_in(rng, 1), (couples,), 0, 1 << 20) % (margin + 1)
    sizes = sizes.at[1:1 + 2 * couples:2].set(donor - passed).at[2:2 + 2 * couples:2].set(taker + passed)
    return sizes[jax.random.permutation(jax.random.fold_in(rng, 2), count)]


def noise(own_key, shape, scale, reach, pieces=(), held_as=jnp.bfloat16):
    values = scale * jax.random.normal(own_key, shape, jnp.float32)
    if pieces:
        values = values * block_levels(own_key, shape, pieces, -0.22, 0.18)
    return jnp.clip(values, -reach, reach).astype(held_as)


def setup_inputs(seed: int = 0) -> dict:
    arg_keys = jax.random.split(jax.random.key(seed), 7)
    return {
        "queries": draw_queries(jax.random.fold_in(arg_keys[6], 71), 0),
        "key_states": draw_key_states(jax.random.fold_in(arg_keys[6], 71), 0),
        "value_states": noise(arg_keys[2], (NT, H, W, D), 1.0, 5.0, ((0, 8), (1, 4))),
        "cotangent": noise(arg_keys[3], (NT, H, W, D), 1.0, 5.0, ((0, 8), (1, 4))),
        "frame_blocks": jnp.searchsorted(jnp.cumsum(uneven(arg_keys[4], BLOCKS, NT, 3, 2)), jnp.arange(NT), side="right").astype(jnp.int32),
        "tile_lists": draw_tile_lists(jax.random.fold_in(arg_keys[6], 71), 0),
    }


MASKED = -1.0e30


def rounded(array_in):
    return lax.optimization_barrier(array_in.astype(jnp.bfloat16)).astype(jnp.float32)


def to_tiles(array_in):
    frames = array_in.shape[0]
    channels = array_in.shape[-1]
    tiled_view = array_in.reshape(frames // TT, TT, NTH, TH, NTW, TW, channels)
    tiled_view = tiled_view.transpose(0, 2, 4, 1, 3, 5, 6)
    return tiled_view.reshape(frames // TT, NTH * NTW, TT * TH * TW, channels)


def from_tiles(tiled_in):
    slab_count = tiled_in.shape[0]
    channels = tiled_in.shape[-1]
    tiled_view = tiled_in.reshape(slab_count, NTH, NTW, TT, TH, TW, channels)
    tiled_view = tiled_view.transpose(0, 3, 1, 4, 2, 5, 6)
    return tiled_view.reshape(slab_count * TT, NTH * TH, NTW * TW, channels)


def block_lookup(lookup_table, slot_ids):
    places = jnp.arange(lookup_table.shape[0], dtype=jnp.int32)
    return jnp.sum(jnp.where(slot_ids[:, None] == places[None, :], lookup_table[None, :], 0), axis=1)


def window_blocks(frame_blocks, slab_index):
    padded = jnp.concatenate([jnp.zeros((2 * TT,), jnp.int32), frame_blocks.astype(jnp.int32)])
    return lax.dynamic_slice_in_dim(padded, (slab_index * TT).astype(jnp.int32), 3 * TT)


def key_mask(listed_ids, slab_index, blocks_here):
    frames = jnp.arange(TT * TH * TW, dtype=jnp.int32) // (TH * TW)
    distance = listed_ids // TPS
    slot_ids = ((2 - distance)[:, None] * TT + frames[None, :]).reshape(-1)
    present = jnp.repeat(slab_index - distance >= 0, TT * TH * TW)
    key_block = block_lookup(blocks_here, slot_ids)
    query_block = block_lookup(blocks_here, 2 * TT + frames)
    return present[None, :] & (key_block[None, :] <= query_block[:, None])


def head_view(array_in):
    return array_in.astype(jnp.float32).reshape(array_in.shape[0], -1, HEAD_DIM)


def reference(queries, key_states, value_states, cotangent, frame_blocks, tile_lists):
    model_width = queries.shape[-1]
    score_scale = HEAD_DIM ** -0.5
    q_all = to_tiles(queries)
    k_all = to_tiles(key_states)
    v_all = to_tiles(value_states)
    c_all = to_tiles(cotangent)
    slab_count = q_all.shape[0]
    zero_slabs = jnp.zeros((2,) + k_all.shape[1:], k_all.dtype)
    k_pad = jnp.concatenate([zero_slabs, k_all])
    v_pad = jnp.concatenate([zero_slabs, v_all])
    zero_sums = jnp.zeros((slab_count + 2,) + k_all.shape[1:], jnp.float32)

    def slab_step(running, slab_index):
        key_sum, value_sum = running
        key_table = jnp.concatenate([lax.dynamic_index_in_dim(k_pad, slab_index + 2 - distance, 0, keepdims=False) for distance in range(3)])
        value_table = jnp.concatenate([lax.dynamic_index_in_dim(v_pad, slab_index + 2 - distance, 0, keepdims=False) for distance in range(3)])
        blocks_here = window_blocks(frame_blocks, slab_index)
        tile_ids = lax.dynamic_index_in_dim(tile_lists, slab_index, 0, keepdims=False).reshape(TPS, K_NB)
        q_slab = lax.dynamic_index_in_dim(q_all, slab_index, 0, keepdims=False)
        c_slab = lax.dynamic_index_in_dim(c_all, slab_index, 0, keepdims=False)

        def tile_step(tables, tile_item):
            q_tile, c_tile, listed_ids = tile_item
            allowed = key_mask(listed_ids, slab_index, blocks_here)
            k_keys = jnp.take(key_table, listed_ids, axis=0).reshape(-1, model_width)
            v_keys = jnp.take(value_table, listed_ids, axis=0).reshape(-1, model_width)
            query_heads = head_view(q_tile)
            key_heads = head_view(k_keys)
            value_heads = head_view(v_keys)
            cot_heads = head_view(c_tile)
            scores = jnp.einsum("qhd,khd->hqk", query_heads, key_heads) * score_scale
            scores = jnp.where(allowed[None], scores, MASKED)
            row_max = jnp.max(scores, axis=-1)
            raised = jnp.exp(scores - row_max[..., None])
            row_sum = jnp.sum(raised, axis=-1)
            weights = rounded(raised / row_sum[..., None])
            attended = jnp.einsum("hqk,khd->qhd", weights, value_heads).reshape(-1, model_width).astype(jnp.bfloat16)
            log_sums = row_max + jnp.log(row_sum)
            back_probs = jnp.exp(scores - log_sums[..., None])
            dprobs = jnp.einsum("qhd,khd->hqk", cot_heads, value_heads)
            row_delta = jnp.sum(cot_heads * head_view(attended), axis=-1).T
            dscores = rounded(back_probs * (dprobs - row_delta[..., None]))
            grad_q = (jnp.einsum("hqk,khd->qhd", dscores, key_heads) * score_scale).reshape(-1, model_width)
            grad_k = jnp.einsum("hqk,qhd->khd", dscores, query_heads) * score_scale
            grad_v = jnp.einsum("hqk,qhd->khd", rounded(back_probs), cot_heads)
            key_tab, value_tab = tables
            key_tab = key_tab.at[listed_ids].add(grad_k.reshape(K_NB, TILE, model_width))
            value_tab = value_tab.at[listed_ids].add(grad_v.reshape(K_NB, TILE, model_width))
            return (key_tab, value_tab), (attended, grad_q.astype(jnp.bfloat16))

        zero_tab = jnp.zeros((3 * TPS, TILE, model_width), jnp.float32)
        (key_tab, value_tab), (attended, grad_q) = lax.scan(tile_step, (zero_tab, zero_tab), (q_slab, c_slab, tile_ids))
        for distance in range(3):
            target = slab_index + 2 - distance
            current = lax.dynamic_index_in_dim(key_sum, target, 0, keepdims=False)
            key_sum = lax.dynamic_update_index_in_dim(key_sum, current + key_tab[distance * TPS:(distance + 1) * TPS], target, 0)
            current = lax.dynamic_index_in_dim(value_sum, target, 0, keepdims=False)
            value_sum = lax.dynamic_update_index_in_dim(value_sum, current + value_tab[distance * TPS:(distance + 1) * TPS], target, 0)
        return (key_sum, value_sum), (attended, grad_q)

    (key_sum, value_sum), (attended, grad_q) = lax.scan(slab_step, (zero_sums, zero_sums), jnp.arange(slab_count, dtype=jnp.int32))
    return (from_tiles(attended), from_tiles(grad_q), from_tiles(key_sum[2:].astype(jnp.bfloat16)), from_tiles(value_sum[2:].astype(jnp.bfloat16)))
```

```python
import functools
import math

import jax
import jax.numpy as jnp
from jax import lax
from jax.experimental import pallas as pl
from jax.experimental.pallas import tpu as pltpu
from jax.sharding import Mesh, PartitionSpec as P

HEAD_DIM = 128
TT = 2
TH = 8
TW = 8
NTW = 2
TPS = 4
K_NB = 10
MASKED = -1e30
CHUNKS = ((0, 2), (2, 2), (4, 1))
VMEM_LIMIT = 48 * 1024 * 1024


def run_copies(copies):
    for copy in copies:
        copy.start()
    for copy in copies:
        copy.wait()


def pack(arrays, members, heads, first, count):
    n = len(arrays)
    tokens = arrays[0].shape[0]
    width = count * HEAD_DIM

    def body(*refs):
        ins, out, sems = refs[:n], refs[n], refs[n + 1]
        run_copies(
            [
                pltpu.make_async_copy(
                    ins[a].at[:, pl.ds((p * heads + first) * HEAD_DIM, width)],
                    out.at[p, a],
                    sems.at[p * n + a],
                )
                for p in range(members)
                for a in range(n)
            ]
        )

    return pl.pallas_call(
        body,
        out_shape=jax.ShapeDtypeStruct((members, n, tokens, width), arrays[0].dtype),
        in_specs=[pl.BlockSpec(memory_space=pl.ANY)] * n,
        out_specs=pl.BlockSpec(memory_space=pl.ANY),
        scratch_shapes=[pltpu.SemaphoreType.DMA((members * n,))],
        cost_estimate=pl.CostEstimate(
            flops=0, bytes_accessed=4 * members * n * tokens * width, transcendentals=0
        ),
        name="pack",
    )(*arrays)


def unpack(received, outputs, shape, heads, first, count):
    members, n, tokens, width = received.shape
    filled = outputs is not None

    def body(*refs):
        source = refs[0]
        outs = refs[1 + n : 1 + 2 * n] if filled else refs[1 : 1 + n]
        sems = refs[-1]
        run_copies(
            [
                pltpu.make_async_copy(
                    source.at[p, a],
                    outs[a].at[:, pl.ds((p * heads + first) * HEAD_DIM, width)],
                    sems.at[p * n + a],
                )
                for p in range(members)
                for a in range(n)
            ]
        )

    args = (received,) + (tuple(outputs) if filled else ())
    return pl.pallas_call(
        body,
        out_shape=[jax.ShapeDtypeStruct(shape, received.dtype)] * n,
        in_specs=[pl.BlockSpec(memory_space=pl.ANY)] * len(args),
        out_specs=[pl.BlockSpec(memory_space=pl.ANY)] * n,
        scratch_shapes=[pltpu.SemaphoreType.DMA((members * n,))],
        input_output_aliases={1 + a: a for a in range(n)} if filled else {},
        cost_estimate=pl.CostEstimate(
            flops=0, bytes_accessed=4 * members * n * tokens * width, transcendentals=0
        ),
        name="unpack",
    )(*args)


def attention_body(
    bias_ref, class_ref, q_ref, c_ref, kc_ref, vc_ref, kp_ref, vp_ref,
    odq_ref, cur_ref, prev_ref, k_all, v_all, dk_all, dv_all,
):
    parts, rows = q_ref.shape[0], q_ref.shape[1]
    plane = parts * rows
    slab = plane // 2
    scale = HEAD_DIM ** -0.5
    scale2 = scale * math.log2(math.e)
    half = parts // 2
    k_all[:plane] = kp_ref[...].reshape(plane, HEAD_DIM)
    k_all[plane:] = kc_ref[...].reshape(plane, HEAD_DIM)
    v_all[:plane] = vp_ref[...].reshape(plane, HEAD_DIM)
    v_all[plane:] = vc_ref[...].reshape(plane, HEAD_DIM)
    dk_all[...] = jnp.zeros_like(dk_all)
    dv_all[...] = jnp.zeros_like(dv_all)
    nt = (((1,), (1,)), ((), ()))
    tn = (((0,), (0,)), ((), ()))
    for y in range(2):
        window = pl.ds(y * slab, 3 * slab)
        for piece in range(2):
            here = pl.ds(y * half + piece * (half // 2), half // 2)
            block = slab // 2
            q = q_ref[here].reshape(block, HEAD_DIM)
            c = c_ref[here].reshape(block, HEAD_DIM)
            k = k_all[window]
            v = v_all[window]
            classes = class_ref[pl.ds(piece * block, block)]
            s = lax.dot_general(
                jnp.concatenate([q, classes], axis=1),
                jnp.concatenate([k, bias_ref[y]], axis=1),
                nt,
                preferred_element_type=jnp.float32,
            )
            m = jnp.max(s, axis=1, keepdims=True)
            e = jnp.exp2((s - m) * scale2)
            p = e * (1.0 / jnp.sum(e, axis=1, keepdims=True))
            w = p.astype(jnp.bfloat16)
            o = jnp.dot(w, v, preferred_element_type=jnp.float32).astype(jnp.bfloat16)
            delta = jnp.sum(
                c.astype(jnp.float32) * o.astype(jnp.float32), axis=1, keepdims=True
            )
            dp = lax.dot_general(c, v, nt, preferred_element_type=jnp.float32)
            ds = (p * (dp - delta)).astype(jnp.bfloat16)
            dq = jnp.dot(ds, k, preferred_element_type=jnp.float32) * scale
            odq_ref[here, 0] = o.reshape(half // 2, rows, HEAD_DIM)
            odq_ref[here, 1] = dq.astype(jnp.bfloat16).reshape(half // 2, rows, HEAD_DIM)
            dk_all[window] += lax.dot_general(ds, q, tn, preferred_element_type=jnp.float32)
            dv_all[window] += lax.dot_general(w, c, tn, preferred_element_type=jnp.float32)
    prev_ref[:, 0] = (dk_all[:plane] * scale).astype(jnp.bfloat16).reshape(kp_ref.shape)
    prev_ref[:, 1] = dv_all[:plane].astype(jnp.bfloat16).reshape(kp_ref.shape)
    cur_ref[:, 0] = (dk_all[plane:] * scale).reshape(kp_ref.shape)
    cur_ref[:, 1] = dv_all[plane:].reshape(kp_ref.shape)


def attention(bias, classes, qc, kv, kv_prev):
    parts, _, rows, width = qc.shape
    plane = parts * rows
    heads = width // HEAD_DIM
    products = heads * 2 * (plane // 2) * 3 * (plane // 2)

    def one(array):
        return pl.BlockSpec(
            (parts, None, rows, HEAD_DIM), lambda h, array=array: (0, array, 0, h)
        )

    both = pl.BlockSpec((parts, 2, rows, HEAD_DIM), lambda h: (0, 0, 0, h))
    return pl.pallas_call(
        attention_body,
        grid=(heads,),
        out_shape=[
            jax.ShapeDtypeStruct(qc.shape, jnp.bfloat16),
            jax.ShapeDtypeStruct(qc.shape, jnp.float32),
            jax.ShapeDtypeStruct(qc.shape, jnp.bfloat16),
        ],
        in_specs=[
            pl.BlockSpec(bias.shape, lambda h: (0, 0, 0)),
            pl.BlockSpec(classes.shape, lambda h: (0, 0)),
            one(0), one(1), one(0), one(1), one(0), one(1),
        ],
        out_specs=[both, both, both],
        scratch_shapes=[
            pltpu.VMEM((2 * plane, HEAD_DIM), jnp.bfloat16),
            pltpu.VMEM((2 * plane, HEAD_DIM), jnp.bfloat16),
            pltpu.VMEM((2 * plane, HEAD_DIM), jnp.float32),
            pltpu.VMEM((2 * plane, HEAD_DIM), jnp.float32),
        ],
        compiler_params=pltpu.CompilerParams(vmem_limit_bytes=VMEM_LIMIT),
        cost_estimate=pl.CostEstimate(
            flops=24 * products * HEAD_DIM,
            bytes_accessed=2 * 9 * qc.size,
            transcendentals=products,
        ),
        name="attention",
    )(bias, classes, qc, qc, kv, kv, kv_prev, kv_prev)


def mask_operands(frame_blocks, tile_lists, z, bands, frame_rows, frame_cols):
    blocks = frame_blocks.reshape(-1, TT)
    padded = jnp.concatenate([jnp.zeros((2, TT), jnp.int32), blocks])
    tile_rows = frame_rows // TH
    lists = lax.dynamic_slice_in_dim(tile_lists, 2 * z, 2).reshape(2, TPS, K_NB)
    near = lax.dynamic_slice_in_dim(padded, 2 * z, 4)
    key_blocks = jnp.stack([near[0:3], near[1:4]])
    query_blocks = near[2:4]
    distance = 2 - jnp.arange(3, dtype=jnp.int32)
    ids = distance[:, None] * TPS + jnp.arange(TPS, dtype=jnp.int32)[None, :]
    listed = jnp.any(lists[:, :, None, None, :] == ids[None, None, :, :, None], axis=-1)
    present = (2 * z + jnp.arange(2, dtype=jnp.int32))[:, None] >= distance[None, :]
    causal = key_blocks[:, :, :, None] <= query_blocks[:, None, None, :]
    allowed = (
        listed.transpose(0, 2, 3, 1)[:, :, :, None, :, None]
        & present[:, :, None, None, None, None]
        & causal[:, :, None, :, None, :]
    )
    table = jnp.where(allowed, 0.0, MASKED).astype(jnp.bfloat16)
    table = table.reshape(2, 3, tile_rows, NTW, TT, TPS * TT)
    table = table.transpose(0, 1, 2, 4, 3, 5)
    table = jnp.pad(table, [(0, 0)] * 5 + [(0, HEAD_DIM - TPS * TT)])
    per_band = frame_rows // bands
    bias = jnp.broadcast_to(
        table[:, :, :, None, :, None, :, None, :],
        (2, 3, tile_rows, bands // tile_rows, TT, per_band, NTW, TW, HEAD_DIM),
    ).reshape(2, -1, HEAD_DIM)
    row = lax.broadcasted_iota(jnp.int32, (bands * TT * per_band * frame_cols, HEAD_DIM), 0)
    lane = lax.broadcasted_iota(jnp.int32, row.shape, 1)
    per_frame = per_band * frame_cols
    band = row // (TT * per_frame)
    frame = row // per_frame % TT
    tile = band // (bands // tile_rows) * NTW + row % frame_cols // TW
    classes = (lane == tile * TT + frame).astype(jnp.bfloat16)
    return bias, classes


def on_device(planes, bands, queries, key_states, value_states, cotangent, frame_blocks, tile_lists):
    members = 2 * bands
    width = queries.shape[-1]
    heads = width // HEAD_DIM // members
    z = lax.axis_index("plane")
    group = ("half", "band")
    q, k, v, c = (
        array.reshape(-1, width) for array in (queries, key_states, value_states, cotangent)
    )
    up = [(i, i + 1) for i in range(planes - 1)]
    down = [(i + 1, i) for i in range(planes - 1)]

    def exchange(array):
        return lax.all_to_all(array, group, split_axis=0, concat_axis=0, tiled=True)

    chunks = [(first, count) for first, count in CHUNKS if first + count <= heads]
    if sum(count for _, count in chunks) != heads:
        chunks = [(0, heads)]
    received = []
    for first, count in chunks:
        kv = exchange(pack((k, v), members, heads, first, count))
        kv_prev = lax.ppermute(kv, "plane", up)
        qc = exchange(pack((q, c), members, heads, first, count))
        received.append((qc, kv, kv_prev))
    bias, classes = mask_operands(
        frame_blocks, tile_lists, z, bands, queries.shape[1] * bands, queries.shape[2]
    )
    out_odq = out_dkv = None
    for (first, count), (qc, kv, kv_prev) in zip(chunks, received):
        odq, dkv, dkv_prev = attention(bias, classes, qc, kv, kv_prev)
        dkv_next = lax.ppermute(dkv_prev, "plane", down)
        out_odq = unpack(exchange(odq), out_odq, q.shape, heads, first, count)
        total = (dkv + dkv_next.astype(jnp.float32)).astype(jnp.bfloat16)
        out_dkv = unpack(exchange(total), out_dkv, q.shape, heads, first, count)
    return tuple(array.reshape(queries.shape) for array in (*out_odq, *out_dkv))


def solution(mesh):
    slabs, bands = mesh.shape["tm"], mesh.shape["band"]
    planes = slabs // 2
    split = Mesh(mesh.devices.reshape(planes, 2, bands), ("plane", "half", "band"))
    rows = P(("plane", "half"), "band", None, None)
    return jax.shard_map(
        functools.partial(on_device, planes, bands),
        mesh=split,
        in_specs=(rows, rows, rows, rows, P(), P()),
        out_specs=(rows, rows, rows, rows),
        check_vma=False,
    )
```

```python
import functools
import math

import jax
import jax.numpy as jnp
from jax import lax
from jax.experimental import pallas as pl
from jax.experimental.pallas import tpu as pltpu
from jax.sharding import Mesh, PartitionSpec as P

HEAD_DIM = 128
TT = 2
TH = 8
TW = 8
NTW = 2
TPS = 4
K_NB = 10
MASKED = -1e30
CHUNKS = ((0, 2), (2, 2), (4, 1))
VMEM_LIMIT = 48 * 1024 * 1024


def pack(arrays, members, heads, chunks):
    n = len(arrays)
    tokens = arrays[0].shape[0]

    def body(*refs):
        ins, outs = refs[:n], refs[n:]
        for (first, count), out in zip(chunks, outs):
            for a in range(n):
                out[0, a] = ins[a][:, first * HEAD_DIM : (first + count) * HEAD_DIM]

    return pl.pallas_call(
        body,
        grid=(members,),
        out_shape=[
            jax.ShapeDtypeStruct((members, n, tokens, count * HEAD_DIM), arrays[0].dtype)
            for _, count in chunks
        ],
        in_specs=[pl.BlockSpec((tokens, heads * HEAD_DIM), lambda p: (0, p))] * n,
        out_specs=[
            pl.BlockSpec((1, n, tokens, count * HEAD_DIM), lambda p: (p, 0, 0, 0))
            for _, count in chunks
        ],
        cost_estimate=pl.CostEstimate(
            flops=0, bytes_accessed=4 * n * arrays[0].size, transcendentals=0
        ),
        name="pack",
    )(*arrays)


def unpack(received, members, heads, chunks):
    n, tokens = received[0].shape[1:3]

    def body(*refs):
        ins, outs = refs[: len(chunks)], refs[len(chunks) :]
        for (first, count), source in zip(chunks, ins):
            for a in range(n):
                outs[a][:, first * HEAD_DIM : (first + count) * HEAD_DIM] = source[0, a]

    shape = (tokens, members * heads * HEAD_DIM)
    return pl.pallas_call(
        body,
        grid=(members,),
        out_shape=[jax.ShapeDtypeStruct(shape, received[0].dtype)] * n,
        in_specs=[
            pl.BlockSpec((1, n, tokens, count * HEAD_DIM), lambda p: (p, 0, 0, 0))
            for _, count in chunks
        ],
        out_specs=[pl.BlockSpec((tokens, heads * HEAD_DIM), lambda p: (0, p))] * n,
        cost_estimate=pl.CostEstimate(
            flops=0, bytes_accessed=4 * n * math.prod(shape), transcendentals=0
        ),
        name="unpack",
    )(*received)


def attention_body(
    bias_ref, class_ref, q_ref, c_ref, kc_ref, vc_ref, kp_ref, vp_ref,
    odq_ref, cur_ref, prev_ref, k_all, v_all, dk_all, dv_all,
):
    parts, rows = q_ref.shape[0], q_ref.shape[1]
    plane = parts * rows
    slab = plane // 2
    scale = HEAD_DIM ** -0.5
    scale2 = scale * math.log2(math.e)
    half = parts // 2
    k_all[:plane] = kp_ref[...].reshape(plane, HEAD_DIM)
    k_all[plane:] = kc_ref[...].reshape(plane, HEAD_DIM)
    v_all[:plane] = vp_ref[...].reshape(plane, HEAD_DIM)
    v_all[plane:] = vc_ref[...].reshape(plane, HEAD_DIM)
    dk_all[...] = jnp.zeros_like(dk_all)
    dv_all[...] = jnp.zeros_like(dv_all)
    nt = (((1,), (1,)), ((), ()))
    tn = (((0,), (0,)), ((), ()))
    for y in range(2):
        window = pl.ds(y * slab, 3 * slab)
        for piece in range(2):
            here = pl.ds(y * half + piece * (half // 2), half // 2)
            block = slab // 2
            q = q_ref[here].reshape(block, HEAD_DIM)
            c = c_ref[here].reshape(block, HEAD_DIM)
            k = k_all[window]
            v = v_all[window]
            classes = class_ref[pl.ds(piece * block, block)]
            s = lax.dot_general(
                jnp.concatenate([q, classes], axis=1),
                jnp.concatenate([k, bias_ref[y]], axis=1),
                nt,
                preferred_element_type=jnp.float32,
            )
            m = jnp.max(s, axis=1, keepdims=True)
            e = jnp.exp2((s - m) * scale2)
            p = e * (1.0 / jnp.sum(e, axis=1, keepdims=True))
            w = p.astype(jnp.bfloat16)
            o = jnp.dot(w, v, preferred_element_type=jnp.float32).astype(jnp.bfloat16)
            delta = jnp.sum(
                c.astype(jnp.float32) * o.astype(jnp.float32), axis=1, keepdims=True
            )
            dp = lax.dot_general(c, v, nt, preferred_element_type=jnp.float32)
            ds = (p * (dp - delta)).astype(jnp.bfloat16)
            dq = jnp.dot(ds, k, preferred_element_type=jnp.float32) * scale
            odq_ref[here, 0] = o.reshape(half // 2, rows, HEAD_DIM)
            odq_ref[here, 1] = dq.astype(jnp.bfloat16).reshape(half // 2, rows, HEAD_DIM)
            dk_all[window] += lax.dot_general(ds, q, tn, preferred_element_type=jnp.float32)
            dv_all[window] += lax.dot_general(w, c, tn, preferred_element_type=jnp.float32)
    prev_ref[:, 0] = (dk_all[:plane] * scale).astype(jnp.bfloat16).reshape(kp_ref.shape)
    prev_ref[:, 1] = dv_all[:plane].astype(jnp.bfloat16).reshape(kp_ref.shape)
    cur_ref[:, 0] = (dk_all[plane:] * scale).reshape(kp_ref.shape)
    cur_ref[:, 1] = dv_all[plane:].reshape(kp_ref.shape)


def attention(bias, classes, qc, kv, kv_prev):
    parts, _, rows, width = qc.shape
    plane = parts * rows
    heads = width // HEAD_DIM
    products = heads * 2 * (plane // 2) * 3 * (plane // 2)

    def one(array):
        return pl.BlockSpec(
            (parts, None, rows, HEAD_DIM), lambda h, array=array: (0, array, 0, h)
        )

    both = pl.BlockSpec((parts, 2, rows, HEAD_DIM), lambda h: (0, 0, 0, h))
    return pl.pallas_call(
        attention_body,
        grid=(heads,),
        out_shape=[
            jax.ShapeDtypeStruct(qc.shape, jnp.bfloat16),
            jax.ShapeDtypeStruct(qc.shape, jnp.float32),
            jax.ShapeDtypeStruct(qc.shape, jnp.bfloat16),
        ],
        in_specs=[
            pl.BlockSpec(bias.shape, lambda h: (0, 0, 0)),
            pl.BlockSpec(classes.shape, lambda h: (0, 0)),
            one(0), one(1), one(0), one(1), one(0), one(1),
        ],
        out_specs=[both, both, both],
        scratch_shapes=[
            pltpu.VMEM((2 * plane, HEAD_DIM), jnp.bfloat16),
            pltpu.VMEM((2 * plane, HEAD_DIM), jnp.bfloat16),
            pltpu.VMEM((2 * plane, HEAD_DIM), jnp.float32),
            pltpu.VMEM((2 * plane, HEAD_DIM), jnp.float32),
        ],
        compiler_params=pltpu.CompilerParams(vmem_limit_bytes=VMEM_LIMIT),
        cost_estimate=pl.CostEstimate(
            flops=24 * products * HEAD_DIM,
            bytes_accessed=2 * 9 * qc.size,
            transcendentals=products,
        ),
        name="attention",
    )(bias, classes, qc, qc, kv, kv, kv_prev, kv_prev)


def mask_operands(frame_blocks, tile_lists, z, bands, frame_rows, frame_cols):
    blocks = frame_blocks.reshape(-1, TT)
    padded = jnp.concatenate([jnp.zeros((2, TT), jnp.int32), blocks])
    tile_rows = frame_rows // TH
    lists = lax.dynamic_slice_in_dim(tile_lists, 2 * z, 2).reshape(2, TPS, K_NB)
    near = lax.dynamic_slice_in_dim(padded, 2 * z, 4)
    key_blocks = jnp.stack([near[0:3], near[1:4]])
    query_blocks = near[2:4]
    distance = 2 - jnp.arange(3, dtype=jnp.int32)
    ids = distance[:, None] * TPS + jnp.arange(TPS, dtype=jnp.int32)[None, :]
    listed = jnp.any(lists[:, :, None, None, :] == ids[None, None, :, :, None], axis=-1)
    present = (2 * z + jnp.arange(2, dtype=jnp.int32))[:, None] >= distance[None, :]
    causal = key_blocks[:, :, :, None] <= query_blocks[:, None, None, :]
    allowed = (
        listed.transpose(0, 2, 3, 1)[:, :, :, None, :, None]
        & present[:, :, None, None, None, None]
        & causal[:, :, None, :, None, :]
    )
    table = jnp.where(allowed, 0.0, MASKED).astype(jnp.bfloat16)
    table = table.reshape(2, 3, tile_rows, NTW, TT, TPS * TT)
    table = table.transpose(0, 1, 2, 4, 3, 5)
    table = jnp.pad(table, [(0, 0)] * 5 + [(0, HEAD_DIM - TPS * TT)])
    per_band = frame_rows // bands
    bias = jnp.broadcast_to(
        table[:, :, :, None, :, None, :, None, :],
        (2, 3, tile_rows, bands // tile_rows, TT, per_band, NTW, TW, HEAD_DIM),
    ).reshape(2, -1, HEAD_DIM)
    row = lax.broadcasted_iota(jnp.int32, (bands * TT * per_band * frame_cols, HEAD_DIM), 0)
    lane = lax.broadcasted_iota(jnp.int32, row.shape, 1)
    per_frame = per_band * frame_cols
    band = row // (TT * per_frame)
    frame = row // per_frame % TT
    tile = band // (bands // tile_rows) * NTW + row % frame_cols // TW
    classes = (lane == tile * TT + frame).astype(jnp.bfloat16)
    return bias, classes


def on_device(planes, bands, queries, key_states, value_states, cotangent, frame_blocks, tile_lists):
    members = 2 * bands
    width = queries.shape[-1]
    heads = width // HEAD_DIM // members
    z = lax.axis_index("plane")
    group = ("half", "band")
    q, k, v, c = (
        array.reshape(-1, width) for array in (queries, key_states, value_states, cotangent)
    )
    up = [(i, i + 1) for i in range(planes - 1)]
    down = [(i + 1, i) for i in range(planes - 1)]

    def exchange(array):
        return lax.all_to_all(array, group, split_axis=0, concat_axis=0, tiled=True)

    chunks = [(first, count) for first, count in CHUNKS if first + count <= heads]
    if sum(count for _, count in chunks) != heads:
        chunks = [(0, heads)]
    kv_sent = pack((k, v), members, heads, chunks)
    qc_sent = pack((q, c), members, heads, chunks)
    received = []
    for kv_part, qc_part in zip(kv_sent, qc_sent):
        kv = exchange(kv_part)
        received.append((exchange(qc_part), kv, lax.ppermute(kv, "plane", up)))
    bias, classes = mask_operands(
        frame_blocks, tile_lists, z, bands, queries.shape[1] * bands, queries.shape[2]
    )
    odq_back, dkv_back = [], []
    for qc, kv, kv_prev in received:
        odq, dkv, dkv_prev = attention(bias, classes, qc, kv, kv_prev)
        dkv_next = lax.ppermute(dkv_prev, "plane", down)
        odq_back.append(exchange(odq))
        total = (dkv + dkv_next.astype(jnp.float32)).astype(jnp.bfloat16)
        dkv_back.append(exchange(total))
    outputs = unpack(odq_back, members, heads, chunks) + unpack(dkv_back, members, heads, chunks)
    return tuple(array.reshape(queries.shape) for array in outputs)


def solution(mesh):
    slabs, bands = mesh.shape["tm"], mesh.shape["band"]
    planes = slabs // 2
    split = Mesh(mesh.devices.reshape(planes, 2, bands), ("plane", "half", "band"))
    rows = P(("plane", "half"), "band", None, None)
    return jax.shard_map(
        functools.partial(on_device, planes, bands),
        mesh=split,
        in_specs=(rows, rows, rows, rows, P(), P()),
        out_specs=(rows, rows, rows, rows),
        check_vma=False,
    )
```

```python
import functools
import math

import jax
import jax.numpy as jnp
from jax import lax
from jax.experimental import pallas as pl
from jax.experimental.pallas import tpu as pltpu
from jax.sharding import Mesh, PartitionSpec as P

HEAD_DIM = 128
TT = 2
TH = 8
TW = 8
NTW = 2
TPS = 4
K_NB = 10
MASKED = -1e30
CHUNKS = (2, 3)
VMEM_LIMIT = 32 * 1024 * 1024


def whole(count):
    return [pl.BlockSpec(memory_space=pltpu.VMEM)] * count


def pack(arrays, members, heads, groups):
    n = len(arrays)
    tokens = arrays[0].shape[0]

    def body(*refs):
        ins, outs = refs[:n], refs[n:]
        for (first, count), out in zip(groups, outs):
            for p in range(members):
                for h in range(count):
                    start = (p * heads + first + h) * HEAD_DIM
                    for a in range(n):
                        out[p, h * n + a] = ins[a][:, start : start + HEAD_DIM]

    return pl.pallas_call(
        body,
        out_shape=[
            jax.ShapeDtypeStruct((members, n * count, tokens, HEAD_DIM), arrays[0].dtype)
            for _, count in groups
        ],
        in_specs=whole(n),
        out_specs=whole(len(groups)),
        compiler_params=pltpu.CompilerParams(vmem_limit_bytes=VMEM_LIMIT),
        cost_estimate=pl.CostEstimate(
            flops=0, bytes_accessed=4 * n * arrays[0].size, transcendentals=0
        ),
        name="pack",
    )(*arrays)


def unpack(received, n, members, heads, groups):
    tokens = received[0].shape[2]

    def body(*refs):
        ins, outs = refs[: len(groups)], refs[len(groups) :]
        for (first, count), source in zip(groups, ins):
            for p in range(members):
                for h in range(count):
                    start = (p * heads + first + h) * HEAD_DIM
                    for a in range(n):
                        outs[a][:, start : start + HEAD_DIM] = source[p, h * n + a]

    shape = (tokens, members * heads * HEAD_DIM)
    return pl.pallas_call(
        body,
        out_shape=[jax.ShapeDtypeStruct(shape, received[0].dtype)] * n,
        in_specs=whole(len(groups)),
        out_specs=whole(n),
        compiler_params=pltpu.CompilerParams(vmem_limit_bytes=VMEM_LIMIT),
        cost_estimate=pl.CostEstimate(
            flops=0, bytes_accessed=4 * n * math.prod(shape), transcendentals=0
        ),
        name="unpack",
    )(*received)


def attention_body(
    bias_ref, class_ref, q_ref, c_ref, kc_ref, vc_ref, kp_ref, vp_ref,
    odq_ref, cur_ref, prev_ref, k_all, v_all, dk_all, dv_all,
):
    parts, rows = q_ref.shape[0], q_ref.shape[1]
    plane = parts * rows
    slab = plane // 2
    scale = HEAD_DIM ** -0.5
    scale2 = scale * math.log2(math.e)
    half = parts // 2
    k_all[:plane] = kp_ref[...].reshape(plane, HEAD_DIM)
    k_all[plane:] = kc_ref[...].reshape(plane, HEAD_DIM)
    v_all[:plane] = vp_ref[...].reshape(plane, HEAD_DIM)
    v_all[plane:] = vc_ref[...].reshape(plane, HEAD_DIM)
    dk_all[...] = jnp.zeros_like(dk_all)
    dv_all[...] = jnp.zeros_like(dv_all)
    nt = (((1,), (1,)), ((), ()))
    tn = (((0,), (0,)), ((), ()))
    for y in range(2):
        window = pl.ds(y * slab, 3 * slab)
        for piece in range(2):
            here = pl.ds(y * half + piece * (half // 2), half // 2)
            block = slab // 2
            q = q_ref[here].reshape(block, HEAD_DIM)
            c = c_ref[here].reshape(block, HEAD_DIM)
            k = k_all[window]
            v = v_all[window]
            classes = class_ref[pl.ds(piece * block, block)]
            s = lax.dot_general(
                jnp.concatenate([q, classes], axis=1),
                jnp.concatenate([k, bias_ref[y]], axis=1),
                nt,
                preferred_element_type=jnp.float32,
            )
            m = jnp.max(s, axis=1, keepdims=True)
            e = jnp.exp2((s - m) * scale2)
            p = e * (1.0 / jnp.sum(e, axis=1, keepdims=True))
            w = p.astype(jnp.bfloat16)
            o = jnp.dot(w, v, preferred_element_type=jnp.float32).astype(jnp.bfloat16)
            delta = jnp.sum(
                c.astype(jnp.float32) * o.astype(jnp.float32), axis=1, keepdims=True
            )
            dp = lax.dot_general(c, v, nt, preferred_element_type=jnp.float32)
            ds = (p * (dp - delta)).astype(jnp.bfloat16)
            dq = jnp.dot(ds, k, preferred_element_type=jnp.float32) * scale
            odq_ref[here, 0] = o.reshape(half // 2, rows, HEAD_DIM)
            odq_ref[here, 1] = dq.astype(jnp.bfloat16).reshape(half // 2, rows, HEAD_DIM)
            dk_all[window] += lax.dot_general(ds, q, tn, preferred_element_type=jnp.float32)
            dv_all[window] += lax.dot_general(w, c, tn, preferred_element_type=jnp.float32)
    prev_ref[:, 0] = (dk_all[:plane] * scale).astype(jnp.bfloat16).reshape(kp_ref.shape)
    prev_ref[:, 1] = dv_all[:plane].astype(jnp.bfloat16).reshape(kp_ref.shape)
    cur_ref[:, 0] = (dk_all[plane:] * scale).reshape(kp_ref.shape)
    cur_ref[:, 1] = dv_all[plane:].reshape(kp_ref.shape)


def attention(bias, classes, qc, kv, kv_prev, first):
    parts, slots, rows, _ = qc.shape
    plane = parts * rows
    heads = slots // 2
    products = heads * 2 * (plane // 2) * 3 * (plane // 2)

    def one(slot):
        return pl.BlockSpec(
            (parts, None, rows, HEAD_DIM), lambda h, slot=slot: (0, 2 * h + slot, 0, 0)
        )

    both = pl.BlockSpec((parts, 2, rows, HEAD_DIM), lambda h: (0, h, 0, 0))
    return pl.pallas_call(
        attention_body,
        grid=(heads,),
        out_shape=[
            jax.ShapeDtypeStruct(qc.shape, jnp.bfloat16),
            jax.ShapeDtypeStruct(qc.shape, jnp.float32),
            jax.ShapeDtypeStruct(qc.shape, jnp.bfloat16),
        ],
        in_specs=[
            pl.BlockSpec(bias.shape, lambda h: (0, 0, 0)),
            pl.BlockSpec(classes.shape, lambda h: (0, 0)),
            one(0), one(1), one(2 * first), one(2 * first + 1), one(0), one(1),
        ],
        out_specs=[both, both, both],
        scratch_shapes=[
            pltpu.VMEM((2 * plane, HEAD_DIM), jnp.bfloat16),
            pltpu.VMEM((2 * plane, HEAD_DIM), jnp.bfloat16),
            pltpu.VMEM((2 * plane, HEAD_DIM), jnp.float32),
            pltpu.VMEM((2 * plane, HEAD_DIM), jnp.float32),
        ],
        compiler_params=pltpu.CompilerParams(vmem_limit_bytes=VMEM_LIMIT),
        cost_estimate=pl.CostEstimate(
            flops=24 * products * HEAD_DIM,
            bytes_accessed=2 * 9 * qc.size,
            transcendentals=products,
        ),
        name="attention",
    )(bias, classes, qc, qc, kv, kv, kv_prev, kv_prev)


def mask_operands(frame_blocks, tile_lists, z, bands, frame_rows, frame_cols):
    blocks = frame_blocks.reshape(-1, TT)
    padded = jnp.concatenate([jnp.zeros((2, TT), jnp.int32), blocks])
    tile_rows = frame_rows // TH
    lists = lax.dynamic_slice_in_dim(tile_lists, 2 * z, 2).reshape(2, TPS, K_NB)
    near = lax.dynamic_slice_in_dim(padded, 2 * z, 4)
    key_blocks = jnp.stack([near[0:3], near[1:4]])
    query_blocks = near[2:4]
    distance = 2 - jnp.arange(3, dtype=jnp.int32)
    ids = distance[:, None] * TPS + jnp.arange(TPS, dtype=jnp.int32)[None, :]
    listed = jnp.any(lists[:, :, None, None, :] == ids[None, None, :, :, None], axis=-1)
    present = (2 * z + jnp.arange(2, dtype=jnp.int32))[:, None] >= distance[None, :]
    causal = key_blocks[:, :, :, None] <= query_blocks[:, None, None, :]
    allowed = (
        listed.transpose(0, 2, 3, 1)[:, :, :, None, :, None]
        & present[:, :, None, None, None, None]
        & causal[:, :, None, :, None, :]
    )
    table = jnp.where(allowed, 0.0, MASKED).astype(jnp.bfloat16)
    table = table.reshape(2, 3, tile_rows, NTW, TT, TPS * TT)
    table = table.transpose(0, 1, 2, 4, 3, 5)
    table = jnp.pad(table, [(0, 0)] * 5 + [(0, HEAD_DIM - TPS * TT)])
    per_band = frame_rows // bands
    bias = jnp.broadcast_to(
        table[:, :, :, None, :, None, :, None, :],
        (2, 3, tile_rows, bands // tile_rows, TT, per_band, NTW, TW, HEAD_DIM),
    ).reshape(2, -1, HEAD_DIM)
    row = lax.broadcasted_iota(jnp.int32, (bands * TT * per_band * frame_cols, HEAD_DIM), 0)
    lane = lax.broadcasted_iota(jnp.int32, row.shape, 1)
    per_frame = per_band * frame_cols
    band = row // (TT * per_frame)
    frame = row // per_frame % TT
    tile = band // (bands // tile_rows) * NTW + row % frame_cols // TW
    classes = (lane == tile * TT + frame).astype(jnp.bfloat16)
    return bias, classes


def on_device(planes, bands, queries, key_states, value_states, cotangent, frame_blocks, tile_lists):
    members = 2 * bands
    width = queries.shape[-1]
    heads = width // HEAD_DIM // members
    z = lax.axis_index("plane")
    group = ("half", "band")
    q, k, v, c = (
        array.reshape(-1, width) for array in (queries, key_states, value_states, cotangent)
    )
    up = [(i, i + 1) for i in range(planes - 1)]
    down = [(i + 1, i) for i in range(planes - 1)]

    last = []

    def exchange(array):
        if last:
            array, _ = lax.optimization_barrier((array, last[-1]))
        last.append(lax.all_to_all(array, group, split_axis=0, concat_axis=0, tiled=True))
        return last[-1]

    counts = CHUNKS if sum(CHUNKS) == heads else (heads,)
    groups = [(sum(counts[:i]), count) for i, count in enumerate(counts)]
    kv_sent = pack((k, v), members, heads, [(0, heads)])[0]
    kv = exchange(kv_sent)
    kv_prev = []
    for first, count in groups:
        moved = kv[:, 2 * first : 2 * (first + count)]
        if kv_prev:
            moved, _ = lax.optimization_barrier((moved, kv_prev[-1]))
        kv_prev.append(lax.ppermute(moved, "plane", up))
    qc = [exchange(sent) for sent in pack((q, c), members, heads, groups)]
    bias, classes = mask_operands(
        frame_blocks, tile_lists, z, bands, queries.shape[1] * bands, queries.shape[2]
    )
    odq_back, dkv_back, waiting = [], [], None
    for i, (first, count) in enumerate(groups):
        odq, dkv, dkv_prev = attention(bias, classes, qc[i], kv, kv_prev[i], first)
        dkv_next = lax.ppermute(dkv_prev, "plane", down)
        if waiting is not None:
            dkv_back.append(exchange(waiting))
        odq_back.append(exchange(odq))
        waiting = (dkv + dkv_next.astype(jnp.float32)).astype(jnp.bfloat16)
    dkv_back.append(exchange(waiting))
    outputs = unpack(odq_back, 2, members, heads, groups)
    outputs += unpack(dkv_back, 2, members, heads, groups)
    return tuple(array.reshape(queries.shape) for array in outputs)


def solution(mesh):
    slabs, bands = mesh.shape["tm"], mesh.shape["band"]
    planes = slabs // 2
    split = Mesh(mesh.devices.reshape(planes, 2, bands), ("plane", "half", "band"))
    rows = P(("plane", "half"), "band", None, None)
    return jax.shard_map(
        functools.partial(on_device, planes, bands),
        mesh=split,
        in_specs=(rows, rows, rows, rows, P(), P()),
        out_specs=(rows, rows, rows, rows),
        check_vma=False,
    )
```

```python
import functools
import math

import jax
import jax.numpy as jnp
from jax import lax
from jax.experimental import pallas as pl
from jax.experimental.pallas import tpu as pltpu
from jax.sharding import Mesh, PartitionSpec as P

HEAD_DIM = 128
TT = 2
TH = 8
TW = 8
NTW = 2
TPS = 4
K_NB = 10
MASKED = -1e30
CHUNKS = (2, 2, 1)
INWARD = ((("kv", 0),), (("kv", 1), ("qc", 0)), (("qc", 1), ("qc", 2), ("kv", 2)))
OUTWARD = ((("o", 0),), (("o", 1),), (("o", 2), ("d", 0)), (("d", 1), ("d", 2)))
VMEM_LIMIT = 32 * 1024 * 1024


STEPS = 2


def hbm(shape, dtype):
    return pltpu.HBM(shape, dtype)


def pack(pairs, members, heads, layouts):
    names = sorted({name for layout in layouts for name, _ in layout})
    arrays = [array for name in names for array in pairs[name]]
    tokens, width = arrays[0].shape
    here = members // STEPS

    def body(*refs):
        ins, outs = refs[: len(arrays)], refs[len(arrays) :]
        for layout, out in zip(layouts, outs):
            for p in range(here):
                for slot, (name, head) in enumerate(layout):
                    start = (p * heads + head) * HEAD_DIM
                    for a in range(2):
                        source = ins[2 * names.index(name) + a]
                        out[p, 2 * slot + a] = source[:, start : start + HEAD_DIM]

    shapes = [(2 * len(layout), tokens, HEAD_DIM) for layout in layouts]
    return pl.pallas_call(
        body,
        grid=(STEPS,),
        out_shape=[hbm((members, *shape), arrays[0].dtype) for shape in shapes],
        in_specs=[pl.BlockSpec((tokens, width // STEPS), lambda i: (0, i))] * len(arrays),
        out_specs=[pl.BlockSpec((here, *shape), lambda i: (i, 0, 0, 0)) for shape in shapes],
        compiler_params=pltpu.CompilerParams(vmem_limit_bytes=VMEM_LIMIT),
        cost_estimate=pl.CostEstimate(
            flops=0, bytes_accessed=4 * sum(array.size for array in arrays), transcendentals=0
        ),
        name="pack",
    )(*arrays)


def unpack(buffers, places, members, heads):
    tokens = buffers[0].shape[2]
    here = members // STEPS

    def body(*refs):
        ins, outs = refs[: len(buffers)], refs[len(buffers) :]
        for p in range(here):
            for head, (buffer, slot) in enumerate(places):
                start = (p * heads + head) * HEAD_DIM
                for a in range(2):
                    outs[a][:, start : start + HEAD_DIM] = ins[buffer][p, slot + a]

    width = members * heads * HEAD_DIM
    return pl.pallas_call(
        body,
        grid=(STEPS,),
        out_shape=[jax.ShapeDtypeStruct((tokens, width), buffers[0].dtype)] * 2,
        in_specs=[
            pl.BlockSpec((here, *buffer.shape[1:]), lambda i: (i, 0, 0, 0)) for buffer in buffers
        ],
        out_specs=[pl.BlockSpec((tokens, width // STEPS), lambda i: (0, i))] * 2,
        compiler_params=pltpu.CompilerParams(vmem_limit_bytes=VMEM_LIMIT),
        cost_estimate=pl.CostEstimate(
            flops=0, bytes_accessed=8 * tokens * width, transcendentals=0
        ),
        name="unpack",
    )(*buffers)


def attention_body(
    bias_ref, class_ref, q_ref, c_ref, kc_ref, vc_ref, kp_ref, vp_ref,
    odq_ref, cur_ref, prev_ref, k_all, v_all, kt_all, vt_all, dk_all, dv_all,
):
    parts, rows = q_ref.shape[0], q_ref.shape[1]
    plane = parts * rows
    slab = plane // 2
    scale = HEAD_DIM ** -0.5
    scale2 = scale * math.log2(math.e)
    half = parts // 2
    quarter = half // 2
    block = quarter * rows
    k_all[:plane] = kp_ref[...].reshape(plane, HEAD_DIM)
    k_all[plane:] = kc_ref[...].reshape(plane, HEAD_DIM)
    v_all[:plane] = vp_ref[...].reshape(plane, HEAD_DIM)
    v_all[plane:] = vc_ref[...].reshape(plane, HEAD_DIM)
    kt_all[...] = k_all[...].T
    vt_all[...] = v_all[...].T
    nt = (((1,), (1,)), ((), ()))
    for y in range(2):
        window = slice(y * slab, (y + 3) * slab)
        for piece in range(2):
            here = pl.ds(y * half + piece * quarter, quarter)
            q = q_ref[here].reshape(block, HEAD_DIM)
            c = c_ref[here].reshape(block, HEAD_DIM)
            classes = class_ref[piece * block : (piece + 1) * block]
            s = lax.dot_general(
                jnp.concatenate([k_all[window], bias_ref[y]], axis=1),
                jnp.concatenate([q, classes], axis=1),
                nt,
                preferred_element_type=jnp.float32,
            )
            m = jnp.max(s, axis=0, keepdims=True)
            e = jnp.exp2((s - m) * scale2)
            p = e * (1.0 / jnp.sum(e, axis=0, keepdims=True))
            w = p.astype(jnp.bfloat16)
            o = jnp.dot(vt_all[:, window], w, preferred_element_type=jnp.float32)
            o = o.astype(jnp.bfloat16).astype(jnp.float32)
            delta = jnp.sum(c.astype(jnp.float32).T * o, axis=0, keepdims=True)
            dp = lax.dot_general(v_all[window], c, nt, preferred_element_type=jnp.float32)
            ds = (p * (dp - delta)).astype(jnp.bfloat16)
            dq = jnp.dot(kt_all[:, window], ds, preferred_element_type=jnp.float32) * scale
            odq_ref[here, 0] = o.T.astype(jnp.bfloat16).reshape(quarter, rows, HEAD_DIM)
            odq_ref[here, 1] = dq.T.astype(jnp.bfloat16).reshape(quarter, rows, HEAD_DIM)
            dk = jnp.dot(ds, q, preferred_element_type=jnp.float32)
            dv = jnp.dot(w, c, preferred_element_type=jnp.float32)
            if y == 0 and piece == 0:
                dk_all[window] = dk
                dv_all[window] = dv
            elif y == 1 and piece == 0:
                dk_all[slab : 3 * slab] += dk[: 2 * slab]
                dv_all[slab : 3 * slab] += dv[: 2 * slab]
                dk_all[3 * slab :] = dk[2 * slab :]
                dv_all[3 * slab :] = dv[2 * slab :]
            else:
                dk_all[window] += dk
                dv_all[window] += dv
    prev_ref[:, 0] = (dk_all[:plane] * scale).astype(jnp.bfloat16).reshape(kp_ref.shape)
    prev_ref[:, 1] = dv_all[:plane].astype(jnp.bfloat16).reshape(kp_ref.shape)
    cur_ref[:, 0] = (dk_all[plane:] * scale).reshape(kp_ref.shape)
    cur_ref[:, 1] = dv_all[plane:].reshape(kp_ref.shape)


def attention(bias, classes, count, qc, kv, kv_prev):
    parts, _, rows, _ = qc[0].shape
    plane = parts * rows
    products = count * 2 * (plane // 2) * 3 * (plane // 2)

    def one(place, a):
        return pl.BlockSpec(
            (parts, None, rows, HEAD_DIM), lambda h: (0, place[1] + 2 * h + a, 0, 0)
        )

    shape = (parts, 2 * count, rows, HEAD_DIM)
    both = pl.BlockSpec((parts, 2, rows, HEAD_DIM), lambda h: (0, h, 0, 0))
    operands = [(place, a) for place in (qc, kv, kv_prev) for a in range(2)]
    return pl.pallas_call(
        attention_body,
        grid=(count,),
        out_shape=[
            hbm(shape, jnp.bfloat16),
            jax.ShapeDtypeStruct(shape, jnp.float32),
            hbm(shape, jnp.bfloat16),
        ],
        in_specs=[
            pl.BlockSpec(bias.shape, lambda h: (0, 0, 0)),
            pl.BlockSpec(classes.shape, lambda h: (0, 0)),
        ] + [one(place, a) for place, a in operands],
        out_specs=[both, both, both],
        scratch_shapes=[
            pltpu.VMEM((2 * plane, HEAD_DIM), jnp.bfloat16),
            pltpu.VMEM((2 * plane, HEAD_DIM), jnp.bfloat16),
            pltpu.VMEM((HEAD_DIM, 2 * plane), jnp.bfloat16),
            pltpu.VMEM((HEAD_DIM, 2 * plane), jnp.bfloat16),
            pltpu.VMEM((2 * plane, HEAD_DIM), jnp.float32),
            pltpu.VMEM((2 * plane, HEAD_DIM), jnp.float32),
        ],
        compiler_params=pltpu.CompilerParams(vmem_limit_bytes=VMEM_LIMIT),
        cost_estimate=pl.CostEstimate(
            flops=24 * products * HEAD_DIM,
            bytes_accessed=18 * math.prod(shape),
            transcendentals=products,
        ),
        name="attention",
    )(bias, classes, *[place[0] for place, _ in operands])


def mask_operands(frame_blocks, tile_lists, z, bands, frame_rows, frame_cols):
    blocks = frame_blocks.reshape(-1, TT)
    padded = jnp.concatenate([jnp.zeros((2, TT), jnp.int32), blocks])
    tile_rows = frame_rows // TH
    lists = lax.dynamic_slice_in_dim(tile_lists, 2 * z, 2).reshape(2, TPS, K_NB)
    near = lax.dynamic_slice_in_dim(padded, 2 * z, 4)
    key_blocks = jnp.stack([near[0:3], near[1:4]])
    query_blocks = near[2:4]
    distance = 2 - jnp.arange(3, dtype=jnp.int32)
    ids = distance[:, None] * TPS + jnp.arange(TPS, dtype=jnp.int32)[None, :]
    listed = jnp.any(lists[:, :, None, None, :] == ids[None, None, :, :, None], axis=-1)
    present = (2 * z + jnp.arange(2, dtype=jnp.int32))[:, None] >= distance[None, :]
    causal = key_blocks[:, :, :, None] <= query_blocks[:, None, None, :]
    allowed = (
        listed.transpose(0, 2, 3, 1)[:, :, :, None, :, None]
        & present[:, :, None, None, None, None]
        & causal[:, :, None, :, None, :]
    )
    table = jnp.where(allowed, 0.0, MASKED).astype(jnp.bfloat16)
    table = table.reshape(2, 3, tile_rows, NTW, TT, TPS * TT)
    table = table.transpose(0, 1, 2, 4, 3, 5)
    table = jnp.pad(table, [(0, 0)] * 5 + [(0, HEAD_DIM - TPS * TT)])
    per_band = frame_rows // bands
    bias = jnp.broadcast_to(
        table[:, :, :, None, :, None, :, None, :],
        (2, 3, tile_rows, bands // tile_rows, TT, per_band, NTW, TW, HEAD_DIM),
    ).reshape(2, -1, HEAD_DIM)
    row = lax.broadcasted_iota(jnp.int32, (bands * TT * per_band * frame_cols, HEAD_DIM), 0)
    lane = lax.broadcasted_iota(jnp.int32, row.shape, 1)
    per_frame = per_band * frame_cols
    band = row // (TT * per_frame)
    frame = row // per_frame % TT
    tile = band // (bands // tile_rows) * NTW + row % frame_cols // TW
    classes = (lane == tile * TT + frame).astype(jnp.bfloat16)
    return bias, classes


def on_device(planes, bands, queries, key_states, value_states, cotangent, frame_blocks, tile_lists):
    members = 2 * bands
    width = queries.shape[-1]
    heads = width // HEAD_DIM // members
    z = lax.axis_index("plane")
    group = ("half", "band")
    q, k, v, c = (
        array.reshape(-1, width) for array in (queries, key_states, value_states, cotangent)
    )
    up = [(i, i + 1) for i in range(planes - 1)]
    down = [(i + 1, i) for i in range(planes - 1)]

    if sum(CHUNKS) == heads:
        counts, inward, outward = CHUNKS, INWARD, OUTWARD
    else:
        counts = (heads,)
        inward, outward = ((("kv", 0),), (("qc", 0),)), ((("o", 0),), (("d", 0),))
    firsts = [sum(counts[:i]) for i in range(len(counts))]
    last = []

    def after(array, other):
        return lax.optimization_barrier((array, other))[0]

    def exchange(array):
        if last:
            array = after(array, last[-1])
        last.append(lax.all_to_all(array, group, split_axis=0, concat_axis=0, tiled=True))
        return last[-1]

    def layout(items):
        return [(name, firsts[i] + h) for name, i in items for h in range(counts[i])]

    pairs = {"kv": (k, v), "qc": (q, c)}
    sent = pack(pairs, members, heads, [layout(inward[0])])
    sent += pack(pairs, members, heads, [layout(items) for items in inward[1:]])
    place, shifted = {}, []
    for items, buffer in zip(inward, sent):
        buffer = exchange(buffer)
        slot = 0
        for name, i in items:
            place[name, i] = (buffer, slot)
            if name == "kv":
                moved = buffer[:, slot : slot + 2 * counts[i]]
                if shifted:
                    moved = after(moved, shifted[-1])
                shifted.append(lax.ppermute(moved, "plane", up))
            slot += 2 * counts[i]
    bias, classes = mask_operands(
        frame_blocks, tile_lists, z, bands, queries.shape[1] * bands, queries.shape[2]
    )
    made, owed = {}, []
    for i, count in enumerate(counts):
        odq, dkv, dkv_prev = attention(
            bias, classes, count, place["qc", i], place["kv", i], (shifted[i], 0)
        )
        made["o", i] = odq
        owed.append((dkv, lax.ppermute(dkv_prev, "plane", down)))
    for i, (dkv, dkv_next) in enumerate(owed):
        if i + 1 < len(owed):
            dkv_next = after(dkv_next, owed[-1][0])
        made["d", i] = (dkv + dkv_next.astype(jnp.float32)).astype(jnp.bfloat16)
    back, found = [], {}
    for items in outward:
        parts = [made[item] for item in items]
        back.append(exchange(jnp.concatenate(parts, axis=1) if len(parts) > 1 else parts[0]))
        for slot, (name, head) in enumerate(layout(items)):
            found[name, head] = (len(back) - 1, 2 * slot)
    outputs = []
    for name in ("o", "d"):
        used = sorted({found[name, head][0] for head in range(heads)})
        places = [(used.index(found[name, h][0]), found[name, h][1]) for h in range(heads)]
        outputs += unpack([back[i] for i in used], places, members, heads)
    return tuple(array.reshape(queries.shape) for array in outputs)


def solution(mesh):
    slabs, bands = mesh.shape["tm"], mesh.shape["band"]
    planes = slabs // 2
    split = Mesh(mesh.devices.reshape(planes, 2, bands), ("plane", "half", "band"))
    rows = P(("plane", "half"), "band", None, None)
    return jax.shard_map(
        functools.partial(on_device, planes, bands),
        mesh=split,
        in_specs=(rows, rows, rows, rows, P(), P()),
        out_specs=(rows, rows, rows, rows),
        check_vma=False,
    )
```

```python
import functools
import math

import jax
import jax.numpy as jnp
from jax import lax
from jax.experimental import pallas as pl
from jax.experimental.pallas import tpu as pltpu
from jax.sharding import Mesh, PartitionSpec as P

HEAD_DIM = 128
TT = 2
TH = 8
TW = 8
NTW = 2
TPS = 4
K_NB = 10
MASKED = -1e30
CHUNKS = (2, 2, 1)
INWARD = ((("kv", 0),), (("kv", 1), ("qc", 0)), (("qc", 1), ("qc", 2), ("kv", 2)))
OUTWARD = ((("o", 0),), (("o", 1),), (("o", 2), ("d", 0)), (("d", 1), ("d", 2)))
VMEM_LIMIT = 32 * 1024 * 1024


STEPS = 2


def hbm(shape, dtype):
    return pltpu.HBM(shape, dtype)


def in_hbm(arrays):
    return [pltpu.with_memory_space_constraint(array, pltpu.HBM) for array in arrays]


def pack(pairs, members, heads, layouts):
    names = sorted({name for layout in layouts for name, _ in layout})
    arrays = [array for name in names for array in pairs[name]]
    tokens, width = arrays[0].shape
    here = members // STEPS

    def body(*refs):
        ins, outs = refs[: len(arrays)], refs[len(arrays) :]
        for layout, out in zip(layouts, outs):
            for p in range(here):
                for slot, (name, head) in enumerate(layout):
                    start = (p * heads + head) * HEAD_DIM
                    for a in range(2):
                        source = ins[2 * names.index(name) + a]
                        out[p, 2 * slot + a] = source[:, start : start + HEAD_DIM]

    shapes = [(2 * len(layout), tokens, HEAD_DIM) for layout in layouts]
    return pl.pallas_call(
        body,
        grid=(STEPS,),
        out_shape=[hbm((members, *shape), arrays[0].dtype) for shape in shapes],
        in_specs=[pl.BlockSpec((tokens, width // STEPS), lambda i: (0, i))] * len(arrays),
        out_specs=[pl.BlockSpec((here, *shape), lambda i: (i, 0, 0, 0)) for shape in shapes],
        compiler_params=pltpu.CompilerParams(vmem_limit_bytes=VMEM_LIMIT),
        cost_estimate=pl.CostEstimate(
            flops=0, bytes_accessed=4 * sum(array.size for array in arrays), transcendentals=0
        ),
        name="pack",
    )(*in_hbm(arrays))


def unpack(buffers, places, members, heads):
    tokens = buffers[0].shape[2]
    here = members // STEPS

    def body(*refs):
        ins, outs = refs[: len(buffers)], refs[len(buffers) :]
        for p in range(here):
            for head, (buffer, slot) in enumerate(places):
                start = (p * heads + head) * HEAD_DIM
                for a in range(2):
                    outs[a][:, start : start + HEAD_DIM] = ins[buffer][p, slot + a]

    width = members * heads * HEAD_DIM
    return pl.pallas_call(
        body,
        grid=(STEPS,),
        out_shape=[jax.ShapeDtypeStruct((tokens, width), buffers[0].dtype)] * 2,
        in_specs=[
            pl.BlockSpec((here, *buffer.shape[1:]), lambda i: (i, 0, 0, 0)) for buffer in buffers
        ],
        out_specs=[pl.BlockSpec((tokens, width // STEPS), lambda i: (0, i))] * 2,
        compiler_params=pltpu.CompilerParams(vmem_limit_bytes=VMEM_LIMIT),
        cost_estimate=pl.CostEstimate(
            flops=0, bytes_accessed=8 * tokens * width, transcendentals=0
        ),
        name="unpack",
    )(*in_hbm(buffers))


def attention_body(
    bias_ref, class_ref, q_ref, c_ref, kc_ref, vc_ref, kp_ref, vp_ref,
    odq_ref, cur_ref, prev_ref, k_all, v_all, dk_all, dv_all,
):
    parts, rows = q_ref.shape[0], q_ref.shape[1]
    plane = parts * rows
    slab = plane // 2
    scale = HEAD_DIM ** -0.5
    scale2 = scale * math.log2(math.e)
    half = parts // 2
    k_all[:plane] = kp_ref[...].reshape(plane, HEAD_DIM)
    k_all[plane:] = kc_ref[...].reshape(plane, HEAD_DIM)
    v_all[:plane] = vp_ref[...].reshape(plane, HEAD_DIM)
    v_all[plane:] = vc_ref[...].reshape(plane, HEAD_DIM)
    nt = (((1,), (1,)), ((), ()))
    tn = (((0,), (0,)), ((), ()))
    for y in range(2):
        window = slice(y * slab, (y + 3) * slab)
        here = pl.ds(y * half, half)
        q = q_ref[here].reshape(slab, HEAD_DIM)
        c = c_ref[here].reshape(slab, HEAD_DIM)
        s = lax.dot_general(
            jnp.concatenate([q, class_ref[...]], axis=1),
            jnp.concatenate([k_all[window], bias_ref[y]], axis=1),
            nt,
            preferred_element_type=jnp.float32,
        )
        m = jnp.max(s, axis=1, keepdims=True)
        e = jnp.exp2((s - m) * scale2)
        p = e * (1.0 / jnp.sum(e, axis=1, keepdims=True))
        w = p.astype(jnp.bfloat16)
        o = jnp.dot(w, v_all[window], preferred_element_type=jnp.float32).astype(jnp.bfloat16)
        delta = jnp.sum(c.astype(jnp.float32) * o.astype(jnp.float32), axis=1, keepdims=True)
        dp = lax.dot_general(c, v_all[window], nt, preferred_element_type=jnp.float32)
        ds = (p * (dp - delta)).astype(jnp.bfloat16)
        dq = jnp.dot(ds, k_all[window], preferred_element_type=jnp.float32) * scale
        odq_ref[here, 0] = o.reshape(half, rows, HEAD_DIM)
        odq_ref[here, 1] = dq.astype(jnp.bfloat16).reshape(half, rows, HEAD_DIM)
        dk = lax.dot_general(ds, q, tn, preferred_element_type=jnp.float32)
        dv = lax.dot_general(w, c, tn, preferred_element_type=jnp.float32)
        if y == 0:
            dk_all[window] = dk
            dv_all[window] = dv
        else:
            dk_all[slab : 3 * slab] += dk[: 2 * slab]
            dv_all[slab : 3 * slab] += dv[: 2 * slab]
            dk_all[3 * slab :] = dk[2 * slab :]
            dv_all[3 * slab :] = dv[2 * slab :]
    prev_ref[:, 0] = (dk_all[:plane] * scale).astype(jnp.bfloat16).reshape(kp_ref.shape)
    prev_ref[:, 1] = dv_all[:plane].astype(jnp.bfloat16).reshape(kp_ref.shape)
    cur_ref[:, 0] = (dk_all[plane:] * scale).reshape(kp_ref.shape)
    cur_ref[:, 1] = dv_all[plane:].reshape(kp_ref.shape)


def attention(bias, classes, count, qc, kv, kv_prev):
    parts, _, rows, _ = qc[0].shape
    plane = parts * rows
    products = count * 2 * (plane // 2) * 3 * (plane // 2)

    def one(place, a):
        return pl.BlockSpec(
            (parts, None, rows, HEAD_DIM), lambda h: (0, place[1] + 2 * h + a, 0, 0)
        )

    shape = (parts, 2 * count, rows, HEAD_DIM)
    both = pl.BlockSpec((parts, 2, rows, HEAD_DIM), lambda h: (0, h, 0, 0))
    operands = [(place, a) for place in (qc, kv, kv_prev) for a in range(2)]
    return pl.pallas_call(
        attention_body,
        grid=(count,),
        out_shape=[
            hbm(shape, jnp.bfloat16),
            hbm(shape, jnp.float32),
            hbm(shape, jnp.bfloat16),
        ],
        in_specs=[
            pl.BlockSpec(bias.shape, lambda h: (0, 0, 0)),
            pl.BlockSpec(classes.shape, lambda h: (0, 0)),
        ] + [one(place, a) for place, a in operands],
        out_specs=[both, both, both],
        scratch_shapes=[
            pltpu.VMEM((2 * plane, HEAD_DIM), jnp.bfloat16),
            pltpu.VMEM((2 * plane, HEAD_DIM), jnp.bfloat16),
            pltpu.VMEM((2 * plane, HEAD_DIM), jnp.float32),
            pltpu.VMEM((2 * plane, HEAD_DIM), jnp.float32),
        ],
        compiler_params=pltpu.CompilerParams(vmem_limit_bytes=VMEM_LIMIT),
        cost_estimate=pl.CostEstimate(
            flops=24 * products * HEAD_DIM,
            bytes_accessed=18 * math.prod(shape),
            transcendentals=products,
        ),
        name="attention",
    )(*in_hbm([bias, classes]), *[place[0] for place, _ in operands])


def mask_operands(frame_blocks, tile_lists, z, bands, frame_rows, frame_cols):
    blocks = frame_blocks.reshape(-1, TT)
    padded = jnp.concatenate([jnp.zeros((2, TT), jnp.int32), blocks])
    tile_rows = frame_rows // TH
    lists = lax.dynamic_slice_in_dim(tile_lists, 2 * z, 2).reshape(2, TPS, K_NB)
    near = lax.dynamic_slice_in_dim(padded, 2 * z, 4)
    key_blocks = jnp.stack([near[0:3], near[1:4]])
    query_blocks = near[2:4]
    distance = 2 - jnp.arange(3, dtype=jnp.int32)
    ids = distance[:, None] * TPS + jnp.arange(TPS, dtype=jnp.int32)[None, :]
    listed = jnp.any(lists[:, :, None, None, :] == ids[None, None, :, :, None], axis=-1)
    present = (2 * z + jnp.arange(2, dtype=jnp.int32))[:, None] >= distance[None, :]
    causal = key_blocks[:, :, :, None] <= query_blocks[:, None, None, :]
    allowed = (
        listed.transpose(0, 2, 3, 1)[:, :, :, None, :, None]
        & present[:, :, None, None, None, None]
        & causal[:, :, None, :, None, :]
    )
    table = jnp.where(allowed, 0.0, MASKED).astype(jnp.bfloat16)
    table = table.reshape(2, 3, tile_rows, NTW, TT, TPS * TT)
    table = table.transpose(0, 1, 2, 4, 3, 5)
    table = jnp.pad(table, [(0, 0)] * 5 + [(0, HEAD_DIM - TPS * TT)])
    per_band = frame_rows // bands
    bias = jnp.broadcast_to(
        table[:, :, :, None, :, None, :, None, :],
        (2, 3, tile_rows, bands // tile_rows, TT, per_band, NTW, TW, HEAD_DIM),
    ).reshape(2, -1, HEAD_DIM)
    row = lax.broadcasted_iota(jnp.int32, (bands * TT * per_band * frame_cols, HEAD_DIM), 0)
    lane = lax.broadcasted_iota(jnp.int32, row.shape, 1)
    per_frame = per_band * frame_cols
    band = row // (TT * per_frame)
    frame = row // per_frame % TT
    tile = band // (bands // tile_rows) * NTW + row % frame_cols // TW
    classes = (lane == tile * TT + frame).astype(jnp.bfloat16)
    return bias, classes


def on_device(planes, bands, queries, key_states, value_states, cotangent, frame_blocks, tile_lists):
    members = 2 * bands
    width = queries.shape[-1]
    heads = width // HEAD_DIM // members
    z = lax.axis_index("plane")
    group = ("half", "band")
    q, k, v, c = (
        array.reshape(-1, width) for array in (queries, key_states, value_states, cotangent)
    )
    up = [(i, i + 1) for i in range(planes - 1)]
    down = [(i + 1, i) for i in range(planes - 1)]

    if sum(CHUNKS) == heads:
        counts, inward, outward = CHUNKS, INWARD, OUTWARD
    else:
        counts = (heads,)
        inward, outward = ((("kv", 0),), (("qc", 0),)), ((("o", 0),), (("d", 0),))
    firsts = [sum(counts[:i]) for i in range(len(counts))]
    last = []

    def after(array, other):
        return lax.optimization_barrier((array, other))[0]

    def exchange(array):
        if last:
            array = after(array, last[-1])
        last.append(lax.all_to_all(array, group, split_axis=0, concat_axis=0, tiled=True))
        return last[-1]

    def layout(items):
        return [(name, firsts[i] + h) for name, i in items for h in range(counts[i])]

    pairs = {"kv": (k, v), "qc": (q, c)}
    sent = pack(pairs, members, heads, [layout(inward[0])])
    sent += pack(pairs, members, heads, [layout(items) for items in inward[1:]])
    bias, classes = mask_operands(
        frame_blocks, tile_lists, z, bands, queries.shape[1] * bands, queries.shape[2]
    )
    place, shifted = {}, []
    for items, buffer in zip(inward, sent):
        if items is inward[-1]:
            buffer = after(buffer, (bias, classes))
        buffer = exchange(buffer)
        slot = 0
        for name, i in items:
            place[name, i] = (buffer, slot)
            if name == "kv":
                moved = buffer[:, slot : slot + 2 * counts[i]]
                if shifted:
                    moved = after(moved, shifted[-1])
                shifted.append(lax.ppermute(moved, "plane", up))
            slot += 2 * counts[i]
    made, owed = {}, []
    for i, count in enumerate(counts):
        odq, dkv, dkv_prev = attention(
            bias, classes, count, place["qc", i], place["kv", i], (shifted[i], 0)
        )
        made["o", i] = odq
        owed.append((dkv, lax.ppermute(dkv_prev, "plane", down)))
    for i, (dkv, dkv_next) in enumerate(owed):
        if i + 1 < len(owed):
            dkv_next = after(dkv_next, owed[-1][0])
        made["d", i] = (dkv + dkv_next.astype(jnp.float32)).astype(jnp.bfloat16)
    back, found = [], {}
    for items in outward:
        parts = [made[item] for item in items]
        back.append(exchange(jnp.concatenate(parts, axis=1) if len(parts) > 1 else parts[0]))
        for slot, (name, head) in enumerate(layout(items)):
            found[name, head] = (len(back) - 1, 2 * slot)
    outputs = []
    for name in ("o", "d"):
        used = sorted({found[name, head][0] for head in range(heads)})
        places = [(used.index(found[name, h][0]), found[name, h][1]) for h in range(heads)]
        outputs += unpack([back[i] for i in used], places, members, heads)
    return tuple(array.reshape(queries.shape) for array in outputs)


def solution(mesh):
    slabs, bands = mesh.shape["tm"], mesh.shape["band"]
    planes = slabs // 2
    split = Mesh(mesh.devices.reshape(planes, 2, bands), ("plane", "half", "band"))
    rows = P(("plane", "half"), "band", None, None)
    return jax.shard_map(
        functools.partial(on_device, planes, bands),
        mesh=split,
        in_specs=(rows, rows, rows, rows, P(), P()),
        out_specs=(rows, rows, rows, rows),
        check_vma=False,
    )
```

```python
import functools
import math

import jax
import jax.numpy as jnp
from jax import lax
from jax.experimental import pallas as pl
from jax.experimental.pallas import tpu as pltpu
from jax.sharding import Mesh, PartitionSpec as P

HEAD_DIM = 128
TT = 2
TH = 8
TW = 8
NTW = 2
TPS = 4
K_NB = 10
MASKED = -1e30
CHUNKS = (2, 2, 1)
INWARD = ((("kv", 0),), (("kv", 1), ("qc", 0), ("kv", 2)), (("qc", 1), ("qc", 2)))
OUTWARD = ((("o", 0),), (("o", 1),), (("o", 2), ("d", 0)), (("d", 1), ("d", 2)))
VMEM_LIMIT = 32 * 1024 * 1024


STEPS = 2


def hbm(shape, dtype):
    return pltpu.HBM(shape, dtype)


def in_hbm(arrays):
    return [pltpu.with_memory_space_constraint(array, pltpu.HBM) for array in arrays]


def pack(pairs, members, heads, layouts):
    names = sorted({name for layout in layouts for name, _ in layout})
    arrays = [array for name in names for array in pairs[name]]
    tokens, width = arrays[0].shape
    here = members // STEPS

    def body(*refs):
        ins, outs = refs[: len(arrays)], refs[len(arrays) :]
        for layout, out in zip(layouts, outs):
            for p in range(here):
                for slot, (name, head) in enumerate(layout):
                    start = (p * heads + head) * HEAD_DIM
                    for a in range(2):
                        source = ins[2 * names.index(name) + a]
                        out[p, 2 * slot + a] = source[:, start : start + HEAD_DIM]

    shapes = [(2 * len(layout), tokens, HEAD_DIM) for layout in layouts]
    return pl.pallas_call(
        body,
        grid=(STEPS,),
        out_shape=[hbm((members, *shape), arrays[0].dtype) for shape in shapes],
        in_specs=[pl.BlockSpec((tokens, width // STEPS), lambda i: (0, i))] * len(arrays),
        out_specs=[pl.BlockSpec((here, *shape), lambda i: (i, 0, 0, 0)) for shape in shapes],
        compiler_params=pltpu.CompilerParams(vmem_limit_bytes=VMEM_LIMIT),
        cost_estimate=pl.CostEstimate(
            flops=0, bytes_accessed=4 * sum(array.size for array in arrays), transcendentals=0
        ),
        name="pack",
    )(*in_hbm(arrays))


def unpack(buffers, places, members, heads):
    tokens = buffers[0].shape[2]
    here = members // STEPS

    def body(*refs):
        ins, outs = refs[: len(buffers)], refs[len(buffers) :]
        for p in range(here):
            for head, (buffer, slot) in enumerate(places):
                start = (p * heads + head) * HEAD_DIM
                for a in range(2):
                    outs[a][:, start : start + HEAD_DIM] = ins[buffer][p, slot + a]

    width = members * heads * HEAD_DIM
    return pl.pallas_call(
        body,
        grid=(STEPS,),
        out_shape=[jax.ShapeDtypeStruct((tokens, width), buffers[0].dtype)] * 2,
        in_specs=[
            pl.BlockSpec((here, *buffer.shape[1:]), lambda i: (i, 0, 0, 0)) for buffer in buffers
        ],
        out_specs=[pl.BlockSpec((tokens, width // STEPS), lambda i: (0, i))] * 2,
        compiler_params=pltpu.CompilerParams(vmem_limit_bytes=VMEM_LIMIT),
        cost_estimate=pl.CostEstimate(
            flops=0, bytes_accessed=8 * tokens * width, transcendentals=0
        ),
        name="unpack",
    )(*buffers)


def attention_body(
    bias_ref, class_ref, q_ref, c_ref, kc_ref, vc_ref, kp_ref, vp_ref,
    odq_ref, cur_ref, prev_ref, k_all, v_all, dk_all, dv_all,
):
    parts, rows = q_ref.shape[0], q_ref.shape[1]
    plane = parts * rows
    slab = plane // 2
    scale = HEAD_DIM ** -0.5
    scale2 = scale * math.log2(math.e)
    half = parts // 2
    k_all[:plane] = kp_ref[...].reshape(plane, HEAD_DIM)
    k_all[plane:] = kc_ref[...].reshape(plane, HEAD_DIM)
    v_all[:plane] = vp_ref[...].reshape(plane, HEAD_DIM)
    v_all[plane:] = vc_ref[...].reshape(plane, HEAD_DIM)
    nt = (((1,), (1,)), ((), ()))
    tn = (((0,), (0,)), ((), ()))
    block = half // 2 * rows
    tile = 2 * HEAD_DIM
    tiles = range(3 * slab // tile)
    blocks = [(y, piece) for y in range(2) for piece in range(2)]

    def queries_of(j):
        y, piece = blocks[j]
        here = pl.ds(y * half + piece * (half // 2), half // 2)
        return q_ref[here].reshape(block, HEAD_DIM), c_ref[here].reshape(block, HEAD_DIM)

    def keys_of(j, t):
        start = blocks[j][0] * slab + t * tile
        return slice(start, start + tile)

    def scores(j, t):
        y, piece = blocks[j]
        q, c = queries_of(j)
        s = lax.dot_general(
            jnp.concatenate([q, class_ref[piece * block : (piece + 1) * block]], axis=1),
            jnp.concatenate(
                [k_all[keys_of(j, t)], bias_ref[y, t * tile : (t + 1) * tile]], axis=1
            ),
            nt,
            preferred_element_type=jnp.float32,
        )
        dp = lax.dot_general(
            c, v_all[keys_of(j, t)], nt, preferred_element_type=jnp.float32
        )
        return s, dp

    def key_grads(j, t, w, ds):
        q, c = queries_of(j)
        dk = lax.dot_general(ds, q, tn, preferred_element_type=jnp.float32)
        dv = lax.dot_general(w, c, tn, preferred_element_type=jnp.float32)
        keys = keys_of(j, t)
        if j == 0 or (j == 2 and keys.start >= 3 * slab):
            dk_all[keys] = dk
            dv_all[keys] = dv
        else:
            dk_all[keys] += dk
            dv_all[keys] += dv

    ready = [scores(0, t) for t in tiles]
    owed = None
    for j, (y, piece) in enumerate(blocks):
        window = slice(y * slab, (y + 3) * slab)
        here = pl.ds(y * half + piece * (half // 2), half // 2)
        _, c = queries_of(j)
        m = functools.reduce(jnp.maximum, [s for s, _ in ready])
        m = jnp.max(m, axis=1, keepdims=True)
        coming, e = [], []
        for t in tiles:
            if j + 1 < len(blocks):
                coming.append(scores(j + 1, t))
            e.append(jnp.exp2((ready[t][0] - m) * scale2))
        r = 1.0 / jnp.sum(functools.reduce(jnp.add, e), axis=1, keepdims=True)
        p, w = [], []
        for t in tiles:
            if owed is not None:
                key_grads(j - 1, t, owed[0][t], owed[1][t])
            p.append(e[t] * r)
            w.append(p[t].astype(jnp.bfloat16))
        o = jnp.dot(
            jnp.concatenate(w, axis=1), v_all[window], preferred_element_type=jnp.float32
        ).astype(jnp.bfloat16)
        delta = jnp.sum(c.astype(jnp.float32) * o.astype(jnp.float32), axis=1, keepdims=True)
        ds = [(p[t] * (ready[t][1] - delta)).astype(jnp.bfloat16) for t in tiles]
        dq = jnp.dot(
            jnp.concatenate(ds, axis=1), k_all[window], preferred_element_type=jnp.float32
        )
        odq_ref[here, 0] = o.reshape(half // 2, rows, HEAD_DIM)
        odq_ref[here, 1] = (dq * scale).astype(jnp.bfloat16).reshape(half // 2, rows, HEAD_DIM)
        ready, owed = coming, (w, ds)
    for t in tiles:
        key_grads(len(blocks) - 1, t, owed[0][t], owed[1][t])
    prev_ref[:, 0] = (dk_all[:plane] * scale).astype(jnp.bfloat16).reshape(kp_ref.shape)
    prev_ref[:, 1] = dv_all[:plane].astype(jnp.bfloat16).reshape(kp_ref.shape)
    cur_ref[:, 0] = (dk_all[plane:] * scale).reshape(kp_ref.shape)
    cur_ref[:, 1] = dv_all[plane:].reshape(kp_ref.shape)


def attention(bias, classes, count, qc, kv, kv_prev):
    parts, _, rows, _ = qc[0].shape
    plane = parts * rows
    products = count * 2 * (plane // 2) * 3 * (plane // 2)

    def one(place, a):
        return pl.BlockSpec(
            (parts, None, rows, HEAD_DIM), lambda h: (0, place[1] + 2 * h + a, 0, 0)
        )

    shape = (parts, 2 * count, rows, HEAD_DIM)
    both = pl.BlockSpec((parts, 2, rows, HEAD_DIM), lambda h: (0, h, 0, 0))
    operands = [(place, a) for place in (qc, kv, kv_prev) for a in range(2)]
    return pl.pallas_call(
        attention_body,
        grid=(count,),
        out_shape=[
            hbm(shape, jnp.bfloat16),
            hbm(shape, jnp.float32),
            hbm(shape, jnp.bfloat16),
        ],
        in_specs=[
            pl.BlockSpec(bias.shape, lambda h: (0, 0, 0)),
            pl.BlockSpec(classes.shape, lambda h: (0, 0)),
        ] + [one(place, a) for place, a in operands],
        out_specs=[both, both, both],
        scratch_shapes=[
            pltpu.VMEM((2 * plane, HEAD_DIM), jnp.bfloat16),
            pltpu.VMEM((2 * plane, HEAD_DIM), jnp.bfloat16),
            pltpu.VMEM((2 * plane, HEAD_DIM), jnp.float32),
            pltpu.VMEM((2 * plane, HEAD_DIM), jnp.float32),
        ],
        compiler_params=pltpu.CompilerParams(vmem_limit_bytes=VMEM_LIMIT),
        cost_estimate=pl.CostEstimate(
            flops=24 * products * HEAD_DIM,
            bytes_accessed=18 * math.prod(shape),
            transcendentals=products,
        ),
        name="attention",
    )(*in_hbm([bias, classes]), *[place[0] for place, _ in operands])


def mask_operands(frame_blocks, tile_lists, z, bands, frame_rows, frame_cols):
    blocks = frame_blocks.reshape(-1, TT)
    padded = jnp.concatenate([jnp.zeros((2, TT), jnp.int32), blocks])
    tile_rows = frame_rows // TH
    lists = lax.dynamic_slice_in_dim(tile_lists, 2 * z, 2).reshape(2, TPS, K_NB)
    near = lax.dynamic_slice_in_dim(padded, 2 * z, 4)
    key_blocks = jnp.stack([near[0:3], near[1:4]])
    query_blocks = near[2:4]
    distance = 2 - jnp.arange(3, dtype=jnp.int32)
    ids = distance[:, None] * TPS + jnp.arange(TPS, dtype=jnp.int32)[None, :]
    listed = jnp.any(lists[:, :, None, None, :] == ids[None, None, :, :, None], axis=-1)
    present = (2 * z + jnp.arange(2, dtype=jnp.int32))[:, None] >= distance[None, :]
    causal = key_blocks[:, :, :, None] <= query_blocks[:, None, None, :]
    allowed = (
        listed.transpose(0, 2, 3, 1)[:, :, :, None, :, None]
        & present[:, :, None, None, None, None]
        & causal[:, :, None, :, None, :]
    )
    table = jnp.where(allowed, 0.0, MASKED).astype(jnp.bfloat16)
    table = table.reshape(2, 3, tile_rows, NTW, TT, TPS * TT)
    table = table.transpose(0, 1, 2, 4, 3, 5)
    table = jnp.pad(table, [(0, 0)] * 5 + [(0, HEAD_DIM - TPS * TT)])
    per_band = frame_rows // bands
    bias = jnp.broadcast_to(
        table[:, :, :, None, :, None, :, None, :],
        (2, 3, tile_rows, bands // tile_rows, TT, per_band, NTW, TW, HEAD_DIM),
    ).reshape(2, -1, HEAD_DIM)
    row = lax.broadcasted_iota(jnp.int32, (bands * TT * per_band * frame_cols, HEAD_DIM), 0)
    lane = lax.broadcasted_iota(jnp.int32, row.shape, 1)
    per_frame = per_band * frame_cols
    band = row // (TT * per_frame)
    frame = row // per_frame % TT
    tile = band // (bands // tile_rows) * NTW + row % frame_cols // TW
    classes = (lane == tile * TT + frame).astype(jnp.bfloat16)
    return bias, classes


def on_device(planes, bands, queries, key_states, value_states, cotangent, frame_blocks, tile_lists):
    members = 2 * bands
    width = queries.shape[-1]
    heads = width // HEAD_DIM // members
    z = lax.axis_index("plane")
    group = ("half", "band")
    q, k, v, c = (
        array.reshape(-1, width) for array in (queries, key_states, value_states, cotangent)
    )
    up = [(i, i + 1) for i in range(planes - 1)]
    down = [(i + 1, i) for i in range(planes - 1)]

    if sum(CHUNKS) == heads:
        counts, inward, outward = CHUNKS, INWARD, OUTWARD
    else:
        counts = (heads,)
        inward, outward = ((("kv", 0),), (("qc", 0),)), ((("o", 0),), (("d", 0),))
    firsts = [sum(counts[:i]) for i in range(len(counts))]
    last = []

    def after(array, other):
        return lax.optimization_barrier((array, other))[0]

    def exchange(array):
        if last:
            array = after(array, last[-1])
        last.append(lax.all_to_all(array, group, split_axis=0, concat_axis=0, tiled=True))
        return last[-1]

    def layout(items):
        return [(name, firsts[i] + h) for name, i in items for h in range(counts[i])]

    pairs = {"kv": (k, v), "qc": (q, c)}
    sent = pack(pairs, members, heads, [layout(inward[0])])
    sent += pack(pairs, members, heads, [layout(items) for items in inward[1:]])
    bias, classes = mask_operands(
        frame_blocks, tile_lists, z, bands, queries.shape[1] * bands, queries.shape[2]
    )
    place, shifted = {}, []
    for items, buffer in zip(inward, sent):
        if items is inward[-1]:
            buffer = after(buffer, (bias, classes))
        buffer = exchange(buffer)
        slot = 0
        for name, i in items:
            place[name, i] = (buffer, slot)
            if name == "kv":
                moved = buffer[:, slot : slot + 2 * counts[i]]
                if shifted:
                    moved = after(moved, shifted[-1])
                shifted.append(lax.ppermute(moved, "plane", up))
            slot += 2 * counts[i]
    made, owed = {}, []
    for i, count in enumerate(counts):
        odq, dkv, dkv_prev = attention(
            bias, classes, count, place["qc", i], place["kv", i], (shifted[i], 0)
        )
        made["o", i] = odq
        owed.append((dkv, lax.ppermute(dkv_prev, "plane", down)))
    for i, (dkv, dkv_next) in enumerate(owed):
        if i + 1 < len(owed):
            dkv_next = after(dkv_next, owed[-1][0])
        made["d", i] = (dkv + dkv_next.astype(jnp.float32)).astype(jnp.bfloat16)
    back, found = [], {}
    for items in outward:
        parts = [made[item] for item in items]
        back.append(exchange(jnp.concatenate(parts, axis=1) if len(parts) > 1 else parts[0]))
        for slot, (name, head) in enumerate(layout(items)):
            found[name, head] = (len(back) - 1, 2 * slot)
    outputs = []
    for name in ("o", "d"):
        used = sorted({found[name, head][0] for head in range(heads)})
        places = [(used.index(found[name, h][0]), found[name, h][1]) for h in range(heads)]
        outputs += unpack([back[i] for i in used], places, members, heads)
    return tuple(array.reshape(queries.shape) for array in outputs)


def solution(mesh):
    slabs, bands = mesh.shape["tm"], mesh.shape["band"]
    planes = slabs // 2
    split = Mesh(mesh.devices.reshape(planes, 2, bands), ("plane", "half", "band"))
    rows = P(("plane", "half"), "band", None, None)
    return jax.shard_map(
        functools.partial(on_device, planes, bands),
        mesh=split,
        in_specs=(rows, rows, rows, rows, P(), P()),
        out_specs=(rows, rows, rows, rows),
        check_vma=False,
    )
```

```python
import functools
import math

import jax
import jax.numpy as jnp
from jax import lax
from jax.experimental import pallas as pl
from jax.experimental.pallas import tpu as pltpu
from jax.sharding import Mesh, PartitionSpec as P

HEAD_DIM = 128
TT = 2
TH = 8
TW = 8
NTW = 2
TPS = 4
K_NB = 10
MASKED = -1e30
CHUNKS = (2, 2, 1)
ORDER = (
    (("kv", 0),),
    (("kv", 1), ("qc", 0)),
    (("kv", 2), ("qc", 1)),
    (("qc", 2), ("o", 0)),
    (("o", 1),),
    (("o", 2), ("d", 0)),
    (("d", 1), ("d", 2)),
)
VMEM_LIMIT = 32 * 1024 * 1024


STEPS = 2


def hbm(shape, dtype):
    return pltpu.HBM(shape, dtype)


def in_hbm(arrays):
    return [pltpu.with_memory_space_constraint(array, pltpu.HBM) for array in arrays]


def pack(pairs, members, heads, layouts):
    names = sorted({name for layout in layouts for name, _ in layout})
    arrays = [array for name in names for array in pairs[name]]
    tokens, width = arrays[0].shape
    here = members // STEPS

    def body(*refs):
        ins, outs = refs[: len(arrays)], refs[len(arrays) :]
        for layout, out in zip(layouts, outs):
            for p in range(here):
                for slot, (name, head) in enumerate(layout):
                    start = (p * heads + head) * HEAD_DIM
                    for a in range(2):
                        source = ins[2 * names.index(name) + a]
                        out[p, 2 * slot + a] = source[:, start : start + HEAD_DIM]

    shapes = [(2 * len(layout), tokens, HEAD_DIM) for layout in layouts]
    return pl.pallas_call(
        body,
        grid=(STEPS,),
        out_shape=[hbm((members, *shape), arrays[0].dtype) for shape in shapes],
        in_specs=[pl.BlockSpec((tokens, width // STEPS), lambda i: (0, i))] * len(arrays),
        out_specs=[pl.BlockSpec((here, *shape), lambda i: (i, 0, 0, 0)) for shape in shapes],
        compiler_params=pltpu.CompilerParams(vmem_limit_bytes=VMEM_LIMIT),
        cost_estimate=pl.CostEstimate(
            flops=0, bytes_accessed=4 * sum(array.size for array in arrays), transcendentals=0
        ),
        name="pack",
    )(*in_hbm(arrays))


def unpack(buffers, places, members, heads):
    tokens = buffers[0].shape[2]
    here = members // STEPS

    def body(*refs):
        ins, outs = refs[: len(buffers)], refs[len(buffers) :]
        for p in range(here):
            for head, (buffer, slot) in enumerate(places):
                start = (p * heads + head) * HEAD_DIM
                for a in range(2):
                    outs[a][:, start : start + HEAD_DIM] = ins[buffer][p, slot + a]

    width = members * heads * HEAD_DIM
    return pl.pallas_call(
        body,
        grid=(STEPS,),
        out_shape=[jax.ShapeDtypeStruct((tokens, width), buffers[0].dtype)] * 2,
        in_specs=[
            pl.BlockSpec((here, *buffer.shape[1:]), lambda i: (i, 0, 0, 0)) for buffer in buffers
        ],
        out_specs=[pl.BlockSpec((tokens, width // STEPS), lambda i: (0, i))] * 2,
        compiler_params=pltpu.CompilerParams(vmem_limit_bytes=VMEM_LIMIT),
        cost_estimate=pl.CostEstimate(
            flops=0, bytes_accessed=8 * tokens * width, transcendentals=0
        ),
        name="unpack",
    )(*buffers)


def attention_body(
    bias_ref, class_ref, q_ref, c_ref, kc_ref, vc_ref, kp_ref, vp_ref,
    odq_ref, cur_ref, prev_ref, k_all, v_all, dk_all, dv_all,
):
    parts, rows = q_ref.shape[0], q_ref.shape[1]
    plane = parts * rows
    slab = plane // 2
    scale = HEAD_DIM ** -0.5
    scale2 = scale * math.log2(math.e)
    half = parts // 2
    k_all[:plane] = kp_ref[...].reshape(plane, HEAD_DIM)
    k_all[plane:] = kc_ref[...].reshape(plane, HEAD_DIM)
    v_all[:plane] = vp_ref[...].reshape(plane, HEAD_DIM)
    v_all[plane:] = vc_ref[...].reshape(plane, HEAD_DIM)
    nt = (((1,), (1,)), ((), ()))
    tn = (((0,), (0,)), ((), ()))
    block = half // 2 * rows
    tile = 2 * HEAD_DIM
    tiles = range(3 * slab // tile)
    blocks = [(y, piece) for y in range(2) for piece in range(2)]

    def queries_of(j):
        y, piece = blocks[j]
        here = pl.ds(y * half + piece * (half // 2), half // 2)
        return q_ref[here].reshape(block, HEAD_DIM), c_ref[here].reshape(block, HEAD_DIM)

    def keys_of(j, t):
        start = blocks[j][0] * slab + t * tile
        return slice(start, start + tile)

    def scores(j, t):
        y, piece = blocks[j]
        q, _ = queries_of(j)
        return lax.dot_general(
            jnp.concatenate([q, class_ref[piece * block : (piece + 1) * block]], axis=1),
            jnp.concatenate(
                [k_all[keys_of(j, t)], bias_ref[y, t * tile : (t + 1) * tile]], axis=1
            ),
            nt,
            preferred_element_type=jnp.float32,
        )

    def key_grads(j, t, w, ds):
        q, c = queries_of(j)
        dk = lax.dot_general(ds, q, tn, preferred_element_type=jnp.float32)
        dv = lax.dot_general(w, c, tn, preferred_element_type=jnp.float32)
        keys = keys_of(j, t)
        if j == 0 or (j == 2 and keys.start >= 3 * slab):
            dk_all[keys] = dk
            dv_all[keys] = dv
        else:
            dk_all[keys] += dk
            dv_all[keys] += dv

    ready, top = [], None
    for t in tiles:
        ready.append(scores(0, t))
        top = ready[t] if top is None else jnp.maximum(top, ready[t])
    owed = None
    for j, (y, piece) in enumerate(blocks):
        window = slice(y * slab, (y + 3) * slab)
        here = pl.ds(y * half + piece * (half // 2), half // 2)
        _, c = queries_of(j)
        m = jnp.max(top, axis=1, keepdims=True)
        coming, e, top, total = [], [], None, None
        for t in tiles:
            if j + 1 < len(blocks):
                coming.append(scores(j + 1, t))
                top = coming[t] if top is None else jnp.maximum(top, coming[t])
            e.append(jnp.exp2((ready[t] - m) * scale2))
            total = e[t] if total is None else total + e[t]
        r = 1.0 / jnp.sum(total, axis=1, keepdims=True)
        w = []
        for t in tiles:
            if owed is not None:
                key_grads(j - 1, t, owed[0][t], owed[1][t])
            w.append((e[t] * r).astype(jnp.bfloat16))
        o = jnp.dot(
            jnp.concatenate(w, axis=1), v_all[window], preferred_element_type=jnp.float32
        ).astype(jnp.bfloat16)
        delta = jnp.sum(c.astype(jnp.float32) * o.astype(jnp.float32), axis=1, keepdims=True)
        ds = []
        for t in tiles:
            dp = lax.dot_general(
                c, v_all[keys_of(j, t)], nt, preferred_element_type=jnp.float32
            )
            ds.append((e[t] * r * (dp - delta)).astype(jnp.bfloat16))
        dq = jnp.dot(
            jnp.concatenate(ds, axis=1), k_all[window], preferred_element_type=jnp.float32
        )
        odq_ref[here, 0] = o.reshape(half // 2, rows, HEAD_DIM)
        odq_ref[here, 1] = (dq * scale).astype(jnp.bfloat16).reshape(half // 2, rows, HEAD_DIM)
        ready, owed = coming, (w, ds)
    for t in tiles:
        key_grads(len(blocks) - 1, t, owed[0][t], owed[1][t])
    prev_ref[:, 0] = (dk_all[:plane] * scale).astype(jnp.bfloat16).reshape(kp_ref.shape)
    prev_ref[:, 1] = dv_all[:plane].astype(jnp.bfloat16).reshape(kp_ref.shape)
    cur_ref[:, 0] = (dk_all[plane:] * scale).reshape(kp_ref.shape)
    cur_ref[:, 1] = dv_all[plane:].reshape(kp_ref.shape)


def attention(bias, classes, count, qc, kv, kv_prev):
    parts, _, rows, _ = qc[0].shape
    plane = parts * rows
    products = count * 2 * (plane // 2) * 3 * (plane // 2)

    def one(place, a):
        return pl.BlockSpec(
            (parts, None, rows, HEAD_DIM), lambda h: (0, place[1] + 2 * h + a, 0, 0)
        )

    shape = (parts, 2 * count, rows, HEAD_DIM)
    both = pl.BlockSpec((parts, 2, rows, HEAD_DIM), lambda h: (0, h, 0, 0))
    operands = [(place, a) for place in (qc, kv, kv_prev) for a in range(2)]
    return pl.pallas_call(
        attention_body,
        grid=(count,),
        out_shape=[
            hbm(shape, jnp.bfloat16),
            hbm(shape, jnp.float32),
            hbm(shape, jnp.bfloat16),
        ],
        in_specs=[
            pl.BlockSpec(bias.shape, lambda h: (0, 0, 0)),
            pl.BlockSpec(classes.shape, lambda h: (0, 0)),
        ] + [one(place, a) for place, a in operands],
        out_specs=[both, both, both],
        scratch_shapes=[
            pltpu.VMEM((2 * plane, HEAD_DIM), jnp.bfloat16),
            pltpu.VMEM((2 * plane, HEAD_DIM), jnp.bfloat16),
            pltpu.VMEM((2 * plane, HEAD_DIM), jnp.float32),
            pltpu.VMEM((2 * plane, HEAD_DIM), jnp.float32),
        ],
        compiler_params=pltpu.CompilerParams(vmem_limit_bytes=VMEM_LIMIT),
        cost_estimate=pl.CostEstimate(
            flops=24 * products * HEAD_DIM,
            bytes_accessed=18 * math.prod(shape),
            transcendentals=products,
        ),
        name="attention",
    )(*in_hbm([bias, classes]), *[place[0] for place, _ in operands])


def mask_operands(frame_blocks, tile_lists, z, bands, frame_rows, frame_cols):
    blocks = frame_blocks.reshape(-1, TT)
    padded = jnp.concatenate([jnp.zeros((2, TT), jnp.int32), blocks])
    tile_rows = frame_rows // TH
    lists = lax.dynamic_slice_in_dim(tile_lists, 2 * z, 2).reshape(2, TPS, K_NB)
    near = lax.dynamic_slice_in_dim(padded, 2 * z, 4)
    key_blocks = jnp.stack([near[0:3], near[1:4]])
    query_blocks = near[2:4]
    distance = 2 - jnp.arange(3, dtype=jnp.int32)
    ids = distance[:, None] * TPS + jnp.arange(TPS, dtype=jnp.int32)[None, :]
    listed = jnp.any(lists[:, :, None, None, :] == ids[None, None, :, :, None], axis=-1)
    present = (2 * z + jnp.arange(2, dtype=jnp.int32))[:, None] >= distance[None, :]
    causal = key_blocks[:, :, :, None] <= query_blocks[:, None, None, :]
    allowed = (
        listed.transpose(0, 2, 3, 1)[:, :, :, None, :, None]
        & present[:, :, None, None, None, None]
        & causal[:, :, None, :, None, :]
    )
    table = jnp.where(allowed, 0.0, MASKED).astype(jnp.bfloat16)
    table = table.reshape(2, 3, tile_rows, NTW, TT, TPS * TT)
    table = table.transpose(0, 1, 2, 4, 3, 5)
    table = jnp.pad(table, [(0, 0)] * 5 + [(0, HEAD_DIM - TPS * TT)])
    per_band = frame_rows // bands
    bias = jnp.broadcast_to(
        table[:, :, :, None, :, None, :, None, :],
        (2, 3, tile_rows, bands // tile_rows, TT, per_band, NTW, TW, HEAD_DIM),
    ).reshape(2, -1, HEAD_DIM)
    row = lax.broadcasted_iota(jnp.int32, (bands * TT * per_band * frame_cols, HEAD_DIM), 0)
    lane = lax.broadcasted_iota(jnp.int32, row.shape, 1)
    per_frame = per_band * frame_cols
    band = row // (TT * per_frame)
    frame = row // per_frame % TT
    tile = band // (bands // tile_rows) * NTW + row % frame_cols // TW
    classes = (lane == tile * TT + frame).astype(jnp.bfloat16)
    return bias, classes


def on_device(planes, bands, queries, key_states, value_states, cotangent, frame_blocks, tile_lists):
    members = 2 * bands
    width = queries.shape[-1]
    heads = width // HEAD_DIM // members
    z = lax.axis_index("plane")
    group = ("half", "band")
    q, k, v, c = (
        array.reshape(-1, width) for array in (queries, key_states, value_states, cotangent)
    )
    up = [(i, i + 1) for i in range(planes - 1)]
    down = [(i + 1, i) for i in range(planes - 1)]

    if sum(CHUNKS) == heads:
        counts, order = CHUNKS, ORDER
    else:
        counts = (heads,)
        order = ((("kv", 0),), (("qc", 0),), (("o", 0),), (("d", 0),))
    firsts = [sum(counts[:i]) for i in range(len(counts))]
    arrived, place, shifted, owed, made = [], {}, [], [], {}

    def after(array, other):
        return lax.optimization_barrier((array, other))[0]

    def layout(items):
        return [(name, firsts[i] + h) for name, i in items for h in range(counts[i])]

    def work_on(i):
        odq, dkv, dkv_prev = attention(
            bias, classes, counts[i], place["qc", i], place["kv", i], (shifted[i], 0)
        )
        made["o", i] = odq
        owed.append((dkv, lax.ppermute(dkv_prev, "plane", down)))

    def returned(i):
        dkv, dkv_next = owed[i]
        if i + 1 < len(owed):
            dkv_next = after(dkv_next, owed[-1][0])
        return (dkv + dkv_next.astype(jnp.float32)).astype(jnp.bfloat16)

    pairs = {"kv": (k, v), "qc": (q, c)}
    inward = [[item for item in items if item[0] in pairs] for items in order]
    sent = pack(pairs, members, heads, [layout(inward[0])])
    sent += pack(pairs, members, heads, [layout(items) for items in inward[1:] if items])
    bias, classes = mask_operands(
        frame_blocks, tile_lists, z, bands, queries.shape[1] * bands, queries.shape[2]
    )
    for step, items in enumerate(order):
        parts = [sent[step]] if inward[step] else []
        for name, i in items[len(inward[step]) :]:
            if name == "o":
                while ("o", i) not in made:
                    work_on(len(owed))
                parts.append(made["o", i])
            else:
                parts.append(returned(i))
        buffer = jnp.concatenate(parts, axis=1) if len(parts) > 1 else parts[0]
        if step == 2:
            buffer = after(buffer, (bias, classes))
        if arrived:
            buffer = after(buffer, arrived[-1])
        buffer = lax.all_to_all(buffer, group, split_axis=0, concat_axis=0, tiled=True)
        arrived.append(buffer)
        slot = 0
        for name, i in items:
            place[name, i] = (buffer, slot)
            if name == "kv":
                moved = buffer[:, slot : slot + 2 * counts[i]]
                shifted.append(lax.ppermute(moved, "plane", up))
            slot += 2 * counts[i]
    outputs = []
    for name in ("o", "d"):
        used, places = [], []
        for i, count in enumerate(counts):
            buffer, slot = place[name, i]
            if not any(buffer is other for other in used):
                used.append(buffer)
            index = [buffer is other for other in used].index(True)
            places += [(index, slot + 2 * h) for h in range(count)]
        outputs += unpack(used, places, members, heads)
    return tuple(array.reshape(queries.shape) for array in outputs)


def solution(mesh):
    slabs, bands = mesh.shape["tm"], mesh.shape["band"]
    planes = slabs // 2
    split = Mesh(mesh.devices.reshape(planes, 2, bands), ("plane", "half", "band"))
    rows = P(("plane", "half"), "band", None, None)
    return jax.shard_map(
        functools.partial(on_device, planes, bands),
        mesh=split,
        in_specs=(rows, rows, rows, rows, P(), P()),
        out_specs=(rows, rows, rows, rows),
        check_vma=False,
    )
```

```python
import functools
import math

import jax
import jax.numpy as jnp
from jax import lax
from jax.experimental import pallas as pl
from jax.experimental.pallas import tpu as pltpu
from jax.sharding import Mesh, PartitionSpec as P

HEAD_DIM = 128
TT = 2
TH = 8
TW = 8
NTW = 2
TPS = 4
K_NB = 10
MASKED = -1e30
CHUNKS = (2, 2, 1)
ORDER = (
    (("kv", 0),),
    (("kv", 1), ("qc", 0)),
    (("kv", 2), ("qc", 1)),
    (("qc", 2), ("o", 0)),
    (("o", 1),),
    (("o", 2), ("d", 0)),
    (("d", 1), ("d", 2)),
)
VMEM_LIMIT = 32 * 1024 * 1024


STEPS = 2


def hbm(shape, dtype):
    return pltpu.HBM(shape, dtype)


def in_hbm(arrays):
    return [pltpu.with_memory_space_constraint(array, pltpu.HBM) for array in arrays]


def pack(pairs, members, heads, layouts, rooms):
    names = sorted({name for layout in layouts for name, _ in layout})
    arrays = [array for name in names for array in pairs[name]]
    tokens, width = arrays[0].shape
    here = members // STEPS

    def body(*refs):
        ins, outs = refs[: len(arrays)], refs[len(arrays) :]
        for layout, out in zip(layouts, outs):
            for p in range(here):
                for slot, (name, head) in enumerate(layout):
                    start = (p * heads + head) * HEAD_DIM
                    for a in range(2):
                        source = ins[2 * names.index(name) + a]
                        out[p, 2 * slot + a] = source[:, start : start + HEAD_DIM]

    shapes = [(2 * len(layout), tokens, HEAD_DIM) for layout in layouts]
    return pl.pallas_call(
        body,
        grid=(STEPS,),
        out_shape=[
            hbm((members, room, tokens, HEAD_DIM), arrays[0].dtype) for room in rooms
        ],
        in_specs=[pl.BlockSpec((tokens, width // STEPS), lambda i: (0, i))] * len(arrays),
        out_specs=[pl.BlockSpec((here, *shape), lambda i: (i, 0, 0, 0)) for shape in shapes],
        compiler_params=pltpu.CompilerParams(vmem_limit_bytes=VMEM_LIMIT),
        cost_estimate=pl.CostEstimate(
            flops=0, bytes_accessed=4 * sum(array.size for array in arrays), transcendentals=0
        ),
        name="pack",
    )(*in_hbm(arrays))


def unpack(buffers, places, members, heads):
    tokens = buffers[0].shape[2]
    here = members // STEPS

    def body(*refs):
        ins, outs = refs[: len(buffers)], refs[len(buffers) :]
        for p in range(here):
            for head, (buffer, slot) in enumerate(places):
                start = (p * heads + head) * HEAD_DIM
                for a in range(2):
                    outs[a][:, start : start + HEAD_DIM] = ins[buffer][p, slot + a]

    width = members * heads * HEAD_DIM
    return pl.pallas_call(
        body,
        grid=(STEPS,),
        out_shape=[jax.ShapeDtypeStruct((tokens, width), buffers[0].dtype)] * 2,
        in_specs=[
            pl.BlockSpec((here, *buffer.shape[1:]), lambda i: (i, 0, 0, 0)) for buffer in buffers
        ],
        out_specs=[pl.BlockSpec((tokens, width // STEPS), lambda i: (0, i))] * 2,
        compiler_params=pltpu.CompilerParams(vmem_limit_bytes=VMEM_LIMIT),
        cost_estimate=pl.CostEstimate(
            flops=0, bytes_accessed=8 * tokens * width, transcendentals=0
        ),
        name="unpack",
    )(*buffers)


def attention_body(
    bias_ref, class_ref, q_ref, c_ref, kc_ref, vc_ref, kp_ref, vp_ref,
    *refs,
):
    odq_ref, cur_ref, prev_ref, k_all, v_all, dk_all, dv_all = refs[-7:]
    parts, rows = q_ref.shape[0], q_ref.shape[1]
    plane = parts * rows
    slab = plane // 2
    scale = HEAD_DIM ** -0.5
    scale2 = scale * math.log2(math.e)
    half = parts // 2
    k_all[:plane] = kp_ref[...].reshape(plane, HEAD_DIM)
    k_all[plane:] = kc_ref[...].reshape(plane, HEAD_DIM)
    v_all[:plane] = vp_ref[...].reshape(plane, HEAD_DIM)
    v_all[plane:] = vc_ref[...].reshape(plane, HEAD_DIM)
    nt = (((1,), (1,)), ((), ()))
    tn = (((0,), (0,)), ((), ()))
    block = half // 2 * rows
    tile = 2 * HEAD_DIM
    tiles = range(3 * slab // tile)
    blocks = [(y, piece) for y in range(2) for piece in range(2)]

    def queries_of(j):
        y, piece = blocks[j]
        here = pl.ds(y * half + piece * (half // 2), half // 2)
        return q_ref[here].reshape(block, HEAD_DIM), c_ref[here].reshape(block, HEAD_DIM)

    def keys_of(j, t):
        start = blocks[j][0] * slab + t * tile
        return slice(start, start + tile)

    def scores(j, t):
        y, piece = blocks[j]
        q, _ = queries_of(j)
        return lax.dot_general(
            jnp.concatenate([q, class_ref[piece * block : (piece + 1) * block]], axis=1),
            jnp.concatenate(
                [k_all[keys_of(j, t)], bias_ref[y, t * tile : (t + 1) * tile]], axis=1
            ),
            nt,
            preferred_element_type=jnp.float32,
        )

    def key_grads(j, t, w, ds):
        q, c = queries_of(j)
        dk = lax.dot_general(ds, q, tn, preferred_element_type=jnp.float32)
        dv = lax.dot_general(w, c, tn, preferred_element_type=jnp.float32)
        keys = keys_of(j, t)
        if j == 0 or (j == 2 and keys.start >= 3 * slab):
            dk_all[keys] = dk
            dv_all[keys] = dv
        else:
            dk_all[keys] += dk
            dv_all[keys] += dv

    ready, top = [], None
    for t in tiles:
        ready.append(scores(0, t))
        top = ready[t] if top is None else jnp.maximum(top, ready[t])
    owed = None
    for j, (y, piece) in enumerate(blocks):
        window = slice(y * slab, (y + 3) * slab)
        here = pl.ds(y * half + piece * (half // 2), half // 2)
        _, c = queries_of(j)
        m = jnp.max(top, axis=1, keepdims=True)
        coming, e, top, total = [], [], None, None
        for t in tiles:
            if j + 1 < len(blocks):
                coming.append(scores(j + 1, t))
                top = coming[t] if top is None else jnp.maximum(top, coming[t])
            e.append(jnp.exp2((ready[t] - m) * scale2))
            total = e[t] if total is None else total + e[t]
        r = 1.0 / jnp.sum(total, axis=1, keepdims=True)
        w = []
        for t in tiles:
            if owed is not None:
                key_grads(j - 1, t, owed[0][t], owed[1][t])
            w.append((e[t] * r).astype(jnp.bfloat16))
        o = jnp.dot(
            jnp.concatenate(w, axis=1), v_all[window], preferred_element_type=jnp.float32
        ).astype(jnp.bfloat16)
        delta = jnp.sum(c.astype(jnp.float32) * o.astype(jnp.float32), axis=1, keepdims=True)
        ds = []
        for t in tiles:
            dp = lax.dot_general(
                c, v_all[keys_of(j, t)], nt, preferred_element_type=jnp.float32
            )
            ds.append((e[t] * r * (dp - delta)).astype(jnp.bfloat16))
        dq = jnp.dot(
            jnp.concatenate(ds, axis=1), k_all[window], preferred_element_type=jnp.float32
        )
        odq_ref[here, 0] = o.reshape(half // 2, rows, HEAD_DIM)
        odq_ref[here, 1] = (dq * scale).astype(jnp.bfloat16).reshape(half // 2, rows, HEAD_DIM)
        ready, owed = coming, (w, ds)
    for t in tiles:
        key_grads(len(blocks) - 1, t, owed[0][t], owed[1][t])
    prev_ref[:, 0] = (dk_all[:plane] * scale).astype(jnp.bfloat16).reshape(kp_ref.shape)
    prev_ref[:, 1] = dv_all[:plane].astype(jnp.bfloat16).reshape(kp_ref.shape)
    cur_ref[:, 0] = (dk_all[plane:] * scale).reshape(kp_ref.shape)
    cur_ref[:, 1] = dv_all[plane:].reshape(kp_ref.shape)


def attention(bias, classes, count, qc, kv, kv_prev, target):
    parts, _, rows, _ = qc[0].shape
    plane = parts * rows
    products = count * 2 * (plane // 2) * 3 * (plane // 2)

    def one(place, a):
        return pl.BlockSpec(
            (parts, None, rows, HEAD_DIM), lambda h: (0, place[1] + 2 * h + a, 0, 0)
        )

    shape = (parts, 2 * count, rows, HEAD_DIM)
    both = pl.BlockSpec((parts, 2, rows, HEAD_DIM), lambda h: (0, h, 0, 0))
    into = both
    if target is not None:
        skip = target[1] // 2
        into = pl.BlockSpec((parts, 2, rows, HEAD_DIM), lambda h: (0, skip + h, 0, 0))
    operands = [(place, a) for place in (qc, kv, kv_prev) for a in range(2)]
    return pl.pallas_call(
        attention_body,
        grid=(count,),
        out_shape=[
            hbm(shape if target is None else target[0].shape, jnp.bfloat16),
            hbm(shape, jnp.float32),
            hbm(shape, jnp.bfloat16),
        ],
        in_specs=[
            pl.BlockSpec(bias.shape, lambda h: (0, 0, 0)),
            pl.BlockSpec(classes.shape, lambda h: (0, 0)),
        ] + [one(place, a) for place, a in operands]
        + ([] if target is None else [pl.BlockSpec(memory_space=pl.ANY)]),
        out_specs=[into, both, both],
        input_output_aliases={} if target is None else {2 + len(operands): 0},
        scratch_shapes=[
            pltpu.VMEM((2 * plane, HEAD_DIM), jnp.bfloat16),
            pltpu.VMEM((2 * plane, HEAD_DIM), jnp.bfloat16),
            pltpu.VMEM((2 * plane, HEAD_DIM), jnp.float32),
            pltpu.VMEM((2 * plane, HEAD_DIM), jnp.float32),
        ],
        compiler_params=pltpu.CompilerParams(vmem_limit_bytes=VMEM_LIMIT),
        cost_estimate=pl.CostEstimate(
            flops=24 * products * HEAD_DIM,
            bytes_accessed=18 * math.prod(shape),
            transcendentals=products,
        ),
        name="attention",
    )(
        *in_hbm([bias, classes] + [place[0] for place, _ in operands[:4]]),
        *[place[0] for place, _ in operands[4:]],
        *([] if target is None else [target[0]]),
    )


def mask_operands(frame_blocks, tile_lists, z, bands, frame_rows, frame_cols):
    blocks = frame_blocks.reshape(-1, TT)
    padded = jnp.concatenate([jnp.zeros((2, TT), jnp.int32), blocks])
    tile_rows = frame_rows // TH
    lists = lax.dynamic_slice_in_dim(tile_lists, 2 * z, 2).reshape(2, TPS, K_NB)
    near = lax.dynamic_slice_in_dim(padded, 2 * z, 4)
    key_blocks = jnp.stack([near[0:3], near[1:4]])
    query_blocks = near[2:4]
    distance = 2 - jnp.arange(3, dtype=jnp.int32)
    ids = distance[:, None] * TPS + jnp.arange(TPS, dtype=jnp.int32)[None, :]
    listed = jnp.any(lists[:, :, None, None, :] == ids[None, None, :, :, None], axis=-1)
    present = (2 * z + jnp.arange(2, dtype=jnp.int32))[:, None] >= distance[None, :]
    causal = key_blocks[:, :, :, None] <= query_blocks[:, None, None, :]
    allowed = (
        listed.transpose(0, 2, 3, 1)[:, :, :, None, :, None]
        & present[:, :, None, None, None, None]
        & causal[:, :, None, :, None, :]
    )
    table = jnp.where(allowed, 0.0, MASKED).astype(jnp.bfloat16)
    table = table.reshape(2, 3, tile_rows, NTW, TT, TPS * TT)
    table = table.transpose(0, 1, 2, 4, 3, 5)
    table = jnp.pad(table, [(0, 0)] * 5 + [(0, HEAD_DIM - TPS * TT)])
    per_band = frame_rows // bands
    bias = jnp.broadcast_to(
        table[:, :, :, None, :, None, :, None, :],
        (2, 3, tile_rows, bands // tile_rows, TT, per_band, NTW, TW, HEAD_DIM),
    ).reshape(2, -1, HEAD_DIM)
    row = lax.broadcasted_iota(jnp.int32, (bands * TT * per_band * frame_cols, HEAD_DIM), 0)
    lane = lax.broadcasted_iota(jnp.int32, row.shape, 1)
    per_frame = per_band * frame_cols
    band = row // (TT * per_frame)
    frame = row // per_frame % TT
    tile = band // (bands // tile_rows) * NTW + row % frame_cols // TW
    classes = (lane == tile * TT + frame).astype(jnp.bfloat16)
    return bias, classes


def on_device(planes, bands, queries, key_states, value_states, cotangent, frame_blocks, tile_lists):
    members = 2 * bands
    width = queries.shape[-1]
    heads = width // HEAD_DIM // members
    z = lax.axis_index("plane")
    group = ("half", "band")
    q, k, v, c = (
        array.reshape(-1, width) for array in (queries, key_states, value_states, cotangent)
    )
    up = [(i, i + 1) for i in range(planes - 1)]
    down = [(i + 1, i) for i in range(planes - 1)]

    if sum(CHUNKS) == heads:
        counts, order = CHUNKS, ORDER
    else:
        counts = (heads,)
        order = ((("kv", 0),), (("qc", 0),), (("o", 0),), (("d", 0),))
    firsts = [sum(counts[:i]) for i in range(len(counts))]
    arrived, place, shifted, owed, made = [], {}, [], [], {}

    def after(array, other):
        return lax.optimization_barrier((array, other))[0]

    def layout(items):
        return [(name, firsts[i] + h) for name, i in items for h in range(counts[i])]

    def work_on(i, target):
        odq, dkv, dkv_prev = attention(
            bias, classes, counts[i], place["qc", i], place["kv", i], (shifted[i], 0), target
        )
        made["o", i] = odq
        owed.append((dkv, lax.ppermute(dkv_prev, "plane", down)))

    def returned(i):
        dkv, dkv_next = owed[i]
        if i + 1 < len(owed):
            dkv_next = after(dkv_next, owed[-1][0])
        return (dkv + dkv_next.astype(jnp.float32)).astype(jnp.bfloat16)

    pairs = {"kv": (k, v), "qc": (q, c)}
    inward = [[item for item in items if item[0] in pairs] for items in order]
    rooms = [sum(2 * counts[i] for _, i in items) for items in order]
    later = [step for step in range(1, len(order)) if inward[step]]
    sent = dict(zip([0], pack(pairs, members, heads, [layout(inward[0])], rooms[:1])))
    sent.update(
        zip(
            later,
            pack(
                pairs, members, heads,
                [layout(inward[step]) for step in later], [rooms[step] for step in later],
            ),
        )
    )
    bias, classes = mask_operands(
        frame_blocks, tile_lists, z, bands, queries.shape[1] * bands, queries.shape[2]
    )
    for step, items in enumerate(order):
        packed, slot, parts = sent.get(step), 2 * len(layout(inward[step])), []
        for name, i in items[len(inward[step]) :]:
            if name == "o":
                while len(owed) <= i:
                    ours = packed is not None and len(owed) == i
                    work_on(len(owed), (packed, slot) if ours else None)
                if packed is None:
                    parts.append(made["o", i])
                else:
                    packed = made["o", i]
            else:
                parts.append(returned(i))
            slot += 2 * counts[i]
        if packed is not None:
            parts.insert(0, packed)
        buffer = jnp.concatenate(parts, axis=1) if len(parts) > 1 else parts[0]
        if step == 2:
            buffer = after(buffer, (bias, classes))
        if arrived:
            buffer = after(buffer, arrived[-1])
        buffer = lax.all_to_all(buffer, group, split_axis=0, concat_axis=0, tiled=True)
        arrived.append(buffer)
        slot = 0
        for name, i in items:
            place[name, i] = (buffer, slot)
            if name == "kv":
                moved = buffer[:, slot : slot + 2 * counts[i]]
                shifted.append(lax.ppermute(moved, "plane", up))
            slot += 2 * counts[i]
    outputs = []
    for name in ("o", "d"):
        used, places = [], []
        for i, count in enumerate(counts):
            buffer, slot = place[name, i]
            if not any(buffer is other for other in used):
                used.append(buffer)
            index = [buffer is other for other in used].index(True)
            places += [(index, slot + 2 * h) for h in range(count)]
        outputs += unpack(used, places, members, heads)
    return tuple(array.reshape(queries.shape) for array in outputs)


def solution(mesh):
    slabs, bands = mesh.shape["tm"], mesh.shape["band"]
    planes = slabs // 2
    split = Mesh(mesh.devices.reshape(planes, 2, bands), ("plane", "half", "band"))
    rows = P(("plane", "half"), "band", None, None)
    return jax.shard_map(
        functools.partial(on_device, planes, bands),
        mesh=split,
        in_specs=(rows, rows, rows, rows, P(), P()),
        out_specs=(rows, rows, rows, rows),
        check_vma=False,
    )
```

```python
import functools
import math

import jax
import jax.numpy as jnp
from jax import lax
from jax.experimental import pallas as pl
from jax.experimental.pallas import tpu as pltpu
from jax.sharding import Mesh, PartitionSpec as P

HEAD_DIM = 128
TT = 2
TH = 8
TW = 8
NTW = 2
TPS = 4
K_NB = 10
MASKED = -1e30
CHUNKS = (2, 2, 1)
ORDER = (
    (("kv", 0),),
    (("kv", 1), ("qc", 0)),
    (("kv", 2), ("qc", 1)),
    (("qc", 2), ("o", 0)),
    (("o", 1),),
    (("o", 2), ("d", 0)),
    (("d", 1), ("d", 2)),
)
VMEM_LIMIT = 32 * 1024 * 1024


STEPS = 2


def hbm(shape, dtype):
    return pltpu.HBM(shape, dtype)


def in_hbm(arrays):
    return [pltpu.with_memory_space_constraint(array, pltpu.HBM) for array in arrays]


def pack(pairs, members, heads, layouts, rooms):
    names = sorted({name for layout in layouts for name, _ in layout})
    arrays = [array for name in names for array in pairs[name]]
    tokens, width = arrays[0].shape
    here = members // STEPS

    def body(*refs):
        ins, outs = refs[: len(arrays)], refs[len(arrays) :]
        for layout, out in zip(layouts, outs):
            for p in range(here):
                for slot, (name, head) in enumerate(layout):
                    start = (p * heads + head) * HEAD_DIM
                    for a in range(2):
                        source = ins[2 * names.index(name) + a]
                        out[p, 2 * slot + a] = source[:, start : start + HEAD_DIM]

    shapes = [(2 * len(layout), tokens, HEAD_DIM) for layout in layouts]
    return pl.pallas_call(
        body,
        grid=(STEPS,),
        out_shape=[
            hbm((members, room, tokens, HEAD_DIM), arrays[0].dtype) for room in rooms
        ],
        in_specs=[pl.BlockSpec((tokens, width // STEPS), lambda i: (0, i))] * len(arrays),
        out_specs=[pl.BlockSpec((here, *shape), lambda i: (i, 0, 0, 0)) for shape in shapes],
        compiler_params=pltpu.CompilerParams(vmem_limit_bytes=VMEM_LIMIT),
        cost_estimate=pl.CostEstimate(
            flops=0, bytes_accessed=4 * sum(array.size for array in arrays), transcendentals=0
        ),
        name="pack",
    )(*in_hbm(arrays))


def unpack(buffers, places, members, heads):
    tokens = buffers[0].shape[2]
    here = members // STEPS

    def body(*refs):
        ins, outs = refs[: len(buffers)], refs[len(buffers) :]
        for p in range(here):
            for head, (buffer, slot) in enumerate(places):
                start = (p * heads + head) * HEAD_DIM
                for a in range(2):
                    outs[a][:, start : start + HEAD_DIM] = ins[buffer][p, slot + a]

    width = members * heads * HEAD_DIM
    return pl.pallas_call(
        body,
        grid=(STEPS,),
        out_shape=[jax.ShapeDtypeStruct((tokens, width), buffers[0].dtype)] * 2,
        in_specs=[
            pl.BlockSpec((here, *buffer.shape[1:]), lambda i: (i, 0, 0, 0)) for buffer in buffers
        ],
        out_specs=[pl.BlockSpec((tokens, width // STEPS), lambda i: (0, i))] * 2,
        compiler_params=pltpu.CompilerParams(vmem_limit_bytes=VMEM_LIMIT),
        cost_estimate=pl.CostEstimate(
            flops=0, bytes_accessed=8 * tokens * width, transcendentals=0
        ),
        name="unpack",
    )(*buffers)


def attention_body(
    bias_ref, class_ref, q_ref, c_ref, kc_ref, vc_ref, kp_ref, vp_ref,
    *refs,
):
    odq_ref, cur_ref, prev_ref, k_all, v_all, dk_all, dv_all = refs[-7:]
    parts, rows = q_ref.shape[0], q_ref.shape[1]
    plane = parts * rows
    slab = plane // 2
    scale = HEAD_DIM ** -0.5
    scale2 = scale * math.log2(math.e)
    half = parts // 2
    k_all[:plane] = kp_ref[...].reshape(plane, HEAD_DIM)
    k_all[plane:] = kc_ref[...].reshape(plane, HEAD_DIM)
    v_all[:plane] = vp_ref[...].reshape(plane, HEAD_DIM)
    v_all[plane:] = vc_ref[...].reshape(plane, HEAD_DIM)
    nt = (((1,), (1,)), ((), ()))
    tn = (((0,), (0,)), ((), ()))
    block = half // 2 * rows
    tile = slab
    tiles = range(3 * slab // tile)
    blocks = [(y, piece) for y in range(2) for piece in range(2)]

    def queries_of(j):
        y, piece = blocks[j]
        here = pl.ds(y * half + piece * (half // 2), half // 2)
        return q_ref[here].reshape(block, HEAD_DIM), c_ref[here].reshape(block, HEAD_DIM)

    def keys_of(j, t):
        start = blocks[j][0] * slab + t * tile
        return slice(start, start + tile)

    def scores(j, t):
        y, piece = blocks[j]
        q, _ = queries_of(j)
        return lax.dot_general(
            jnp.concatenate([q, class_ref[piece * block : (piece + 1) * block]], axis=1),
            jnp.concatenate(
                [k_all[keys_of(j, t)], bias_ref[y, t * tile : (t + 1) * tile]], axis=1
            ),
            nt,
            preferred_element_type=jnp.float32,
        )

    def key_grads(j, t, w, ds):
        q, c = queries_of(j)
        dk = lax.dot_general(ds, q, tn, preferred_element_type=jnp.float32)
        dv = lax.dot_general(w, c, tn, preferred_element_type=jnp.float32)
        keys = keys_of(j, t)
        if j == 0 or (j == 2 and keys.start >= 3 * slab):
            dk_all[keys] = dk
            dv_all[keys] = dv
        else:
            dk_all[keys] += dk
            dv_all[keys] += dv

    ready, top = [], None
    for t in tiles:
        ready.append(scores(0, t))
        top = ready[t] if top is None else jnp.maximum(top, ready[t])
    owed = None
    for j, (y, piece) in enumerate(blocks):
        window = slice(y * slab, (y + 3) * slab)
        here = pl.ds(y * half + piece * (half // 2), half // 2)
        _, c = queries_of(j)
        m = jnp.max(top, axis=1, keepdims=True)
        coming, e, top, total = [], [], None, None
        for t in tiles:
            if j + 1 < len(blocks):
                coming.append(scores(j + 1, t))
                top = coming[t] if top is None else jnp.maximum(top, coming[t])
            e.append(jnp.exp2((ready[t] - m) * scale2))
            total = e[t] if total is None else total + e[t]
        r = 1.0 / jnp.sum(total, axis=1, keepdims=True)
        w = []
        for t in tiles:
            if owed is not None:
                key_grads(j - 1, t, owed[0][t], owed[1][t])
            w.append((e[t] * r).astype(jnp.bfloat16))
        o = jnp.dot(
            jnp.concatenate(w, axis=1), v_all[window], preferred_element_type=jnp.float32
        ).astype(jnp.bfloat16)
        delta = jnp.sum(c.astype(jnp.float32) * o.astype(jnp.float32), axis=1, keepdims=True)
        ds = []
        for t in tiles:
            dp = lax.dot_general(
                c, v_all[keys_of(j, t)], nt, preferred_element_type=jnp.float32
            )
            ds.append((e[t] * r * (dp - delta)).astype(jnp.bfloat16))
        dq = jnp.dot(
            jnp.concatenate(ds, axis=1), k_all[window], preferred_element_type=jnp.float32
        )
        odq_ref[here, 0] = o.reshape(half // 2, rows, HEAD_DIM)
        odq_ref[here, 1] = (dq * scale).astype(jnp.bfloat16).reshape(half // 2, rows, HEAD_DIM)
        ready, owed = coming, (w, ds)
    for t in tiles:
        key_grads(len(blocks) - 1, t, owed[0][t], owed[1][t])
    prev_ref[:, 0] = (dk_all[:plane] * scale).astype(jnp.bfloat16).reshape(kp_ref.shape)
    prev_ref[:, 1] = dv_all[:plane].astype(jnp.bfloat16).reshape(kp_ref.shape)
    cur_ref[:, 0] = (dk_all[plane:] * scale).reshape(kp_ref.shape)
    cur_ref[:, 1] = dv_all[plane:].reshape(kp_ref.shape)


def attention(bias, classes, count, qc, kv, kv_prev, target):
    parts, _, rows, _ = qc[0].shape
    plane = parts * rows
    products = count * 2 * (plane // 2) * 3 * (plane // 2)

    def one(place, a):
        return pl.BlockSpec(
            (parts, None, rows, HEAD_DIM), lambda h: (0, place[1] + 2 * h + a, 0, 0)
        )

    shape = (parts, 2 * count, rows, HEAD_DIM)
    both = pl.BlockSpec((parts, 2, rows, HEAD_DIM), lambda h: (0, h, 0, 0))
    into = both
    if target is not None:
        skip = target[1] // 2
        into = pl.BlockSpec((parts, 2, rows, HEAD_DIM), lambda h: (0, skip + h, 0, 0))
    operands = [(place, a) for place in (qc, kv, kv_prev) for a in range(2)]
    alone = kv[0].shape[1] == 2 * count
    held = [(place, place is qc or (place is kv and not alone)) for place, _ in operands]
    return pl.pallas_call(
        attention_body,
        grid=(count,),
        out_shape=[
            hbm(shape if target is None else target[0].shape, jnp.bfloat16),
            hbm(shape, jnp.float32),
            hbm(shape, jnp.bfloat16),
        ],
        in_specs=[
            pl.BlockSpec(bias.shape, lambda h: (0, 0, 0)),
            pl.BlockSpec(classes.shape, lambda h: (0, 0)),
        ] + [one(place, a) for place, a in operands]
        + ([] if target is None else [pl.BlockSpec(memory_space=pl.ANY)]),
        out_specs=[into, both, both],
        input_output_aliases={} if target is None else {2 + len(operands): 0},
        scratch_shapes=[
            pltpu.VMEM((2 * plane, HEAD_DIM), jnp.bfloat16),
            pltpu.VMEM((2 * plane, HEAD_DIM), jnp.bfloat16),
            pltpu.VMEM((2 * plane, HEAD_DIM), jnp.float32),
            pltpu.VMEM((2 * plane, HEAD_DIM), jnp.float32),
        ],
        compiler_params=pltpu.CompilerParams(vmem_limit_bytes=VMEM_LIMIT),
        cost_estimate=pl.CostEstimate(
            flops=24 * products * HEAD_DIM,
            bytes_accessed=18 * math.prod(shape),
            transcendentals=products,
        ),
        name="attention",
    )(
        *in_hbm([bias, classes]),
        *[in_hbm([place[0]])[0] if pinned else place[0] for place, pinned in held],
        *([] if target is None else [target[0]]),
    )


def mask_operands(frame_blocks, tile_lists, z, bands, frame_rows, frame_cols):
    blocks = frame_blocks.reshape(-1, TT)
    padded = jnp.concatenate([jnp.zeros((2, TT), jnp.int32), blocks])
    tile_rows = frame_rows // TH
    lists = lax.dynamic_slice_in_dim(tile_lists, 2 * z, 2).reshape(2, TPS, K_NB)
    near = lax.dynamic_slice_in_dim(padded, 2 * z, 4)
    key_blocks = jnp.stack([near[0:3], near[1:4]])
    query_blocks = near[2:4]
    distance = 2 - jnp.arange(3, dtype=jnp.int32)
    ids = distance[:, None] * TPS + jnp.arange(TPS, dtype=jnp.int32)[None, :]
    listed = jnp.any(lists[:, :, None, None, :] == ids[None, None, :, :, None], axis=-1)
    present = (2 * z + jnp.arange(2, dtype=jnp.int32))[:, None] >= distance[None, :]
    causal = key_blocks[:, :, :, None] <= query_blocks[:, None, None, :]
    allowed = (
        listed.transpose(0, 2, 3, 1)[:, :, :, None, :, None]
        & present[:, :, None, None, None, None]
        & causal[:, :, None, :, None, :]
    )
    table = jnp.where(allowed, 0.0, MASKED).astype(jnp.bfloat16)
    table = table.reshape(2, 3, tile_rows, NTW, TT, TPS * TT)
    table = table.transpose(0, 1, 2, 4, 3, 5)
    table = jnp.pad(table, [(0, 0)] * 5 + [(0, HEAD_DIM - TPS * TT)])
    per_band = frame_rows // bands
    bias = jnp.broadcast_to(
        table[:, :, :, None, :, None, :, None, :],
        (2, 3, tile_rows, bands // tile_rows, TT, per_band, NTW, TW, HEAD_DIM),
    ).reshape(2, -1, HEAD_DIM)
    row = lax.broadcasted_iota(jnp.int32, (bands * TT * per_band * frame_cols, HEAD_DIM), 0)
    lane = lax.broadcasted_iota(jnp.int32, row.shape, 1)
    per_frame = per_band * frame_cols
    band = row // (TT * per_frame)
    frame = row // per_frame % TT
    tile = band // (bands // tile_rows) * NTW + row % frame_cols // TW
    classes = (lane == tile * TT + frame).astype(jnp.bfloat16)
    return bias, classes


def on_device(planes, bands, queries, key_states, value_states, cotangent, frame_blocks, tile_lists):
    members = 2 * bands
    width = queries.shape[-1]
    heads = width // HEAD_DIM // members
    z = lax.axis_index("plane")
    group = ("half", "band")
    q, k, v, c = (
        array.reshape(-1, width) for array in (queries, key_states, value_states, cotangent)
    )
    up = [(i, i + 1) for i in range(planes - 1)]
    down = [(i + 1, i) for i in range(planes - 1)]

    if sum(CHUNKS) == heads:
        counts, order = CHUNKS, ORDER
    else:
        counts = (heads,)
        order = ((("kv", 0),), (("qc", 0),), (("o", 0),), (("d", 0),))
    firsts = [sum(counts[:i]) for i in range(len(counts))]
    arrived, place, shifted, owed, made = [], {}, [], [], {}

    def after(array, other):
        return lax.optimization_barrier((array, other))[0]

    def layout(items):
        return [(name, firsts[i] + h) for name, i in items for h in range(counts[i])]

    def work_on(i, target):
        odq, dkv, dkv_prev = attention(
            bias, classes, counts[i], place["qc", i], place["kv", i], (shifted[i], 0), target
        )
        made["o", i] = odq
        owed.append((dkv, lax.ppermute(dkv_prev, "plane", down)))

    def returned(i):
        dkv, dkv_next = owed[i]
        if i + 1 < len(owed):
            dkv_next = after(dkv_next, owed[-1][0])
        return (dkv + dkv_next.astype(jnp.float32)).astype(jnp.bfloat16)

    pairs = {"kv": (k, v), "qc": (q, c)}
    inward = [[item for item in items if item[0] in pairs] for items in order]
    rooms = [sum(2 * counts[i] for _, i in items) for items in order]
    later = [step for step in range(1, len(order)) if inward[step]]
    sent = dict(zip([0], pack(pairs, members, heads, [layout(inward[0])], rooms[:1])))
    sent.update(
        zip(
            later,
            pack(
                pairs, members, heads,
                [layout(inward[step]) for step in later], [rooms[step] for step in later],
            ),
        )
    )
    bias, classes = mask_operands(
        frame_blocks, tile_lists, z, bands, queries.shape[1] * bands, queries.shape[2]
    )
    for step, items in enumerate(order):
        packed, slot, parts = sent.get(step), 2 * len(layout(inward[step])), []
        for name, i in items[len(inward[step]) :]:
            if name == "o":
                while len(owed) <= i:
                    ours = packed is not None and len(owed) == i
                    work_on(len(owed), (packed, slot) if ours else None)
                if packed is None:
                    parts.append(made["o", i])
                else:
                    packed = made["o", i]
            else:
                parts.append(returned(i))
            slot += 2 * counts[i]
        if packed is not None:
            parts.insert(0, packed)
        buffer = jnp.concatenate(parts, axis=1) if len(parts) > 1 else parts[0]
        if step == 2:
            buffer = after(buffer, (bias, classes))
        if arrived:
            buffer = after(buffer, arrived[-1])
        buffer = lax.all_to_all(buffer, group, split_axis=0, concat_axis=0, tiled=True)
        arrived.append(buffer)
        slot = 0
        for name, i in items:
            place[name, i] = (buffer, slot)
            if name == "kv":
                moved = buffer[:, slot : slot + 2 * counts[i]]
                shifted.append(lax.ppermute(moved, "plane", up))
            slot += 2 * counts[i]
    outputs = []
    for name in ("o", "d"):
        used, places = [], []
        for i, count in enumerate(counts):
            buffer, slot = place[name, i]
            if not any(buffer is other for other in used):
                used.append(buffer)
            index = [buffer is other for other in used].index(True)
            places += [(index, slot + 2 * h) for h in range(count)]
        outputs += unpack(used, places, members, heads)
    return tuple(array.reshape(queries.shape) for array in outputs)


def solution(mesh):
    slabs, bands = mesh.shape["tm"], mesh.shape["band"]
    planes = slabs // 2
    split = Mesh(mesh.devices.reshape(planes, 2, bands), ("plane", "half", "band"))
    rows = P(("plane", "half"), "band", None, None)
    return jax.shard_map(
        functools.partial(on_device, planes, bands),
        mesh=split,
        in_specs=(rows, rows, rows, rows, P(), P()),
        out_specs=(rows, rows, rows, rows),
        check_vma=False,
    )
```

```python
import functools
import math

import jax
import jax.numpy as jnp
from jax import lax
from jax.experimental import pallas as pl
from jax.experimental.pallas import tpu as pltpu
from jax.sharding import Mesh, PartitionSpec as P

HEAD_DIM = 128
TT = 2
TH = 8
TW = 8
NTW = 2
TPS = 4
K_NB = 10
MASKED = -1e30
CHUNKS = (2, 1, 2)
ORDER = (
    (("kv", 0),),
    (("kv", 1), ("qc", 0)),
    (("kv", 2), ("qc", 1)),
    (("qc", 2), ("o", 0)),
    (("o", 1), ("d", 0)),
    (("o", 2), ("d", 1)),
    (("d", 2),),
)
VMEM_LIMIT = 32 * 1024 * 1024


STEPS = 2


def hbm(shape, dtype):
    return pltpu.HBM(shape, dtype)


def in_hbm(arrays):
    return [pltpu.with_memory_space_constraint(array, pltpu.HBM) for array in arrays]


def pack(pairs, members, heads, layouts, rooms):
    names = sorted({name for layout in layouts for name, _ in layout})
    arrays = [array for name in names for array in pairs[name]]
    tokens, width = arrays[0].shape
    here = members // STEPS

    def body(*refs):
        ins, outs = refs[: len(arrays)], refs[len(arrays) :]
        for layout, out in zip(layouts, outs):
            for p in range(here):
                for slot, (name, head) in enumerate(layout):
                    start = (p * heads + head) * HEAD_DIM
                    for a in range(2):
                        source = ins[2 * names.index(name) + a]
                        out[p, 2 * slot + a] = source[:, start : start + HEAD_DIM]

    shapes = [(2 * len(layout), tokens, HEAD_DIM) for layout in layouts]
    return pl.pallas_call(
        body,
        grid=(STEPS,),
        out_shape=[
            hbm((members, room, tokens, HEAD_DIM), arrays[0].dtype) for room in rooms
        ],
        in_specs=[pl.BlockSpec((tokens, width // STEPS), lambda i: (0, i))] * len(arrays),
        out_specs=[pl.BlockSpec((here, *shape), lambda i: (i, 0, 0, 0)) for shape in shapes],
        compiler_params=pltpu.CompilerParams(vmem_limit_bytes=VMEM_LIMIT),
        cost_estimate=pl.CostEstimate(
            flops=0, bytes_accessed=4 * sum(array.size for array in arrays), transcendentals=0
        ),
        name="pack",
    )(*in_hbm(arrays))


def unpack(buffers, places, members, heads):
    tokens = buffers[0].shape[2]
    here = members // STEPS

    def body(*refs):
        ins, outs = refs[: len(buffers)], refs[len(buffers) :]
        for p in range(here):
            for head, (buffer, slot) in enumerate(places):
                start = (p * heads + head) * HEAD_DIM
                for a in range(2):
                    outs[a][:, start : start + HEAD_DIM] = ins[buffer][p, slot + a]

    width = members * heads * HEAD_DIM
    return pl.pallas_call(
        body,
        grid=(STEPS,),
        out_shape=[jax.ShapeDtypeStruct((tokens, width), buffers[0].dtype)] * 2,
        in_specs=[
            pl.BlockSpec((here, *buffer.shape[1:]), lambda i: (i, 0, 0, 0)) for buffer in buffers
        ],
        out_specs=[pl.BlockSpec((tokens, width // STEPS), lambda i: (0, i))] * 2,
        compiler_params=pltpu.CompilerParams(vmem_limit_bytes=VMEM_LIMIT),
        cost_estimate=pl.CostEstimate(
            flops=0, bytes_accessed=8 * tokens * width, transcendentals=0
        ),
        name="unpack",
    )(*buffers)


def attention_body(
    bias_ref, class_ref, q_ref, c_ref, kc_ref, vc_ref, kp_ref, vp_ref,
    *refs,
):
    odq_ref, cur_ref, prev_ref, k_all, v_all, dk_all, dv_all = refs[-7:]
    parts, rows = q_ref.shape[0], q_ref.shape[1]
    plane = parts * rows
    slab = plane // 2
    scale = HEAD_DIM ** -0.5
    scale2 = scale * math.log2(math.e)
    half = parts // 2
    k_all[:plane] = kp_ref[...].reshape(plane, HEAD_DIM)
    k_all[plane:] = kc_ref[...].reshape(plane, HEAD_DIM)
    v_all[:plane] = vp_ref[...].reshape(plane, HEAD_DIM)
    v_all[plane:] = vc_ref[...].reshape(plane, HEAD_DIM)
    nt = (((1,), (1,)), ((), ()))
    tn = (((0,), (0,)), ((), ()))
    block = half // 2 * rows
    tile = slab
    tiles = range(3 * slab // tile)
    blocks = [(y, piece) for y in range(2) for piece in range(2)]

    def queries_of(j):
        y, piece = blocks[j]
        here = pl.ds(y * half + piece * (half // 2), half // 2)
        return q_ref[here].reshape(block, HEAD_DIM), c_ref[here].reshape(block, HEAD_DIM)

    def keys_of(j, t):
        start = blocks[j][0] * slab + t * tile
        return slice(start, start + tile)

    def scores(j, t):
        y, piece = blocks[j]
        q, _ = queries_of(j)
        return lax.dot_general(
            jnp.concatenate([q, class_ref[piece * block : (piece + 1) * block]], axis=1),
            jnp.concatenate(
                [k_all[keys_of(j, t)], bias_ref[y, t * tile : (t + 1) * tile]], axis=1
            ),
            nt,
            preferred_element_type=jnp.float32,
        )

    def key_grads(j, t, w, ds):
        q, c = queries_of(j)
        dk = lax.dot_general(ds, q, tn, preferred_element_type=jnp.float32)
        dv = lax.dot_general(w, c, tn, preferred_element_type=jnp.float32)
        keys = keys_of(j, t)
        if j == 0 or (j == 2 and keys.start >= 3 * slab):
            dk_all[keys] = dk
            dv_all[keys] = dv
        else:
            dk_all[keys] += dk
            dv_all[keys] += dv

    ready, top = [], None
    for t in tiles:
        ready.append(scores(0, t))
        top = ready[t] if top is None else jnp.maximum(top, ready[t])
    owed = None
    for j, (y, piece) in enumerate(blocks):
        window = slice(y * slab, (y + 3) * slab)
        here = pl.ds(y * half + piece * (half // 2), half // 2)
        _, c = queries_of(j)
        m = jnp.max(top, axis=1, keepdims=True)
        coming, e, top, total = [], [], None, None
        for t in tiles:
            if j + 1 < len(blocks):
                coming.append(scores(j + 1, t))
                top = coming[t] if top is None else jnp.maximum(top, coming[t])
            e.append(jnp.exp2((ready[t] - m) * scale2))
            total = e[t] if total is None else total + e[t]
        r = 1.0 / jnp.sum(total, axis=1, keepdims=True)
        w = []
        for t in tiles:
            if owed is not None:
                key_grads(j - 1, t, owed[0][t], owed[1][t])
            w.append((e[t] * r).astype(jnp.bfloat16))
        o = jnp.dot(
            jnp.concatenate(w, axis=1), v_all[window], preferred_element_type=jnp.float32
        ).astype(jnp.bfloat16)
        delta = jnp.sum(c.astype(jnp.float32) * o.astype(jnp.float32), axis=1, keepdims=True)
        ds = []
        for t in tiles:
            dp = lax.dot_general(
                c, v_all[keys_of(j, t)], nt, preferred_element_type=jnp.float32
            )
            ds.append((e[t] * r * (dp - delta)).astype(jnp.bfloat16))
        dq = jnp.dot(
            jnp.concatenate(ds, axis=1), k_all[window], preferred_element_type=jnp.float32
        )
        odq_ref[here, 0] = o.reshape(half // 2, rows, HEAD_DIM)
        odq_ref[here, 1] = (dq * scale).astype(jnp.bfloat16).reshape(half // 2, rows, HEAD_DIM)
        ready, owed = coming, (w, ds)
    for t in tiles:
        key_grads(len(blocks) - 1, t, owed[0][t], owed[1][t])
    prev_ref[:, 0] = (dk_all[:plane] * scale).astype(jnp.bfloat16).reshape(kp_ref.shape)
    prev_ref[:, 1] = dv_all[:plane].astype(jnp.bfloat16).reshape(kp_ref.shape)
    cur_ref[:, 0] = (dk_all[plane:] * scale).reshape(kp_ref.shape)
    cur_ref[:, 1] = dv_all[plane:].reshape(kp_ref.shape)


def attention(bias, classes, count, qc, kv, kv_prev, target):
    parts, _, rows, _ = qc[0].shape
    plane = parts * rows
    products = count * 2 * (plane // 2) * 3 * (plane // 2)

    def one(place, a):
        return pl.BlockSpec(
            (parts, None, rows, HEAD_DIM), lambda h: (0, place[1] + 2 * h + a, 0, 0)
        )

    shape = (parts, 2 * count, rows, HEAD_DIM)
    both = pl.BlockSpec((parts, 2, rows, HEAD_DIM), lambda h: (0, h, 0, 0))
    into = both
    if target is not None:
        skip = target[1] // 2
        into = pl.BlockSpec((parts, 2, rows, HEAD_DIM), lambda h: (0, skip + h, 0, 0))
    operands = [(place, a) for place in (qc, kv, kv_prev) for a in range(2)]
    alone = kv[0].shape[1] == 2 * count
    held = [(place, place is qc or (place is kv and not alone)) for place, _ in operands]
    return pl.pallas_call(
        attention_body,
        grid=(count,),
        out_shape=[
            hbm(shape if target is None else target[0].shape, jnp.bfloat16),
            hbm(shape, jnp.float32),
            hbm(shape, jnp.bfloat16),
        ],
        in_specs=[
            pl.BlockSpec(bias.shape, lambda h: (0, 0, 0)),
            pl.BlockSpec(classes.shape, lambda h: (0, 0)),
        ] + [one(place, a) for place, a in operands]
        + ([] if target is None else [pl.BlockSpec(memory_space=pl.ANY)]),
        out_specs=[into, both, both],
        input_output_aliases={} if target is None else {2 + len(operands): 0},
        scratch_shapes=[
            pltpu.VMEM((2 * plane, HEAD_DIM), jnp.bfloat16),
            pltpu.VMEM((2 * plane, HEAD_DIM), jnp.bfloat16),
            pltpu.VMEM((2 * plane, HEAD_DIM), jnp.float32),
            pltpu.VMEM((2 * plane, HEAD_DIM), jnp.float32),
        ],
        compiler_params=pltpu.CompilerParams(vmem_limit_bytes=VMEM_LIMIT),
        cost_estimate=pl.CostEstimate(
            flops=24 * products * HEAD_DIM,
            bytes_accessed=18 * math.prod(shape),
            transcendentals=products,
        ),
        name="attention",
    )(
        *in_hbm([bias, classes]),
        *[in_hbm([place[0]])[0] if pinned else place[0] for place, pinned in held],
        *([] if target is None else [target[0]]),
    )


def mask_operands(frame_blocks, tile_lists, z, bands, frame_rows, frame_cols):
    blocks = frame_blocks.reshape(-1, TT)
    padded = jnp.concatenate([jnp.zeros((2, TT), jnp.int32), blocks])
    tile_rows = frame_rows // TH
    lists = lax.dynamic_slice_in_dim(tile_lists, 2 * z, 2).reshape(2, TPS, K_NB)
    near = lax.dynamic_slice_in_dim(padded, 2 * z, 4)
    key_blocks = jnp.stack([near[0:3], near[1:4]])
    query_blocks = near[2:4]
    distance = 2 - jnp.arange(3, dtype=jnp.int32)
    ids = distance[:, None] * TPS + jnp.arange(TPS, dtype=jnp.int32)[None, :]
    listed = jnp.any(lists[:, :, None, None, :] == ids[None, None, :, :, None], axis=-1)
    present = (2 * z + jnp.arange(2, dtype=jnp.int32))[:, None] >= distance[None, :]
    causal = key_blocks[:, :, :, None] <= query_blocks[:, None, None, :]
    allowed = (
        listed.transpose(0, 2, 3, 1)[:, :, :, None, :, None]
        & present[:, :, None, None, None, None]
        & causal[:, :, None, :, None, :]
    )
    table = jnp.where(allowed, 0.0, MASKED).astype(jnp.bfloat16)
    table = table.reshape(2, 3, tile_rows, NTW, TT, TPS * TT)
    table = table.transpose(0, 1, 2, 4, 3, 5)
    table = jnp.pad(table, [(0, 0)] * 5 + [(0, HEAD_DIM - TPS * TT)])
    per_band = frame_rows // bands
    bias = jnp.broadcast_to(
        table[:, :, :, None, :, None, :, None, :],
        (2, 3, tile_rows, bands // tile_rows, TT, per_band, NTW, TW, HEAD_DIM),
    ).reshape(2, -1, HEAD_DIM)
    row = lax.broadcasted_iota(jnp.int32, (bands * TT * per_band * frame_cols, HEAD_DIM), 0)
    lane = lax.broadcasted_iota(jnp.int32, row.shape, 1)
    per_frame = per_band * frame_cols
    band = row // (TT * per_frame)
    frame = row // per_frame % TT
    tile = band // (bands // tile_rows) * NTW + row % frame_cols // TW
    classes = (lane == tile * TT + frame).astype(jnp.bfloat16)
    return bias, classes


def on_device(planes, bands, queries, key_states, value_states, cotangent, frame_blocks, tile_lists):
    members = 2 * bands
    width = queries.shape[-1]
    heads = width // HEAD_DIM // members
    z = lax.axis_index("plane")
    group = ("half", "band")
    q, k, v, c = (
        array.reshape(-1, width) for array in (queries, key_states, value_states, cotangent)
    )
    up = [(i, i + 1) for i in range(planes - 1)]
    down = [(i + 1, i) for i in range(planes - 1)]

    if sum(CHUNKS) == heads:
        counts, order = CHUNKS, ORDER
    else:
        counts = (heads,)
        order = ((("kv", 0),), (("qc", 0),), (("o", 0),), (("d", 0),))
    firsts = [sum(counts[:i]) for i in range(len(counts))]
    arrived, place, shifted, owed, made = [], {}, [], [], {}

    def after(array, other):
        return lax.optimization_barrier((array, other))[0]

    def layout(items):
        return [(name, firsts[i] + h) for name, i in items for h in range(counts[i])]

    def work_on(i, target):
        odq, dkv, dkv_prev = attention(
            bias, classes, counts[i], place["qc", i], place["kv", i], (shifted[i], 0), target
        )
        made["o", i] = odq
        owed.append((dkv, lax.ppermute(dkv_prev, "plane", down)))

    def returned(i):
        dkv, dkv_next = owed[i]
        if i + 1 < len(owed):
            dkv_next = after(dkv_next, owed[-1][0])
        return (dkv + dkv_next.astype(jnp.float32)).astype(jnp.bfloat16)

    pairs = {"kv": (k, v), "qc": (q, c)}
    inward = [[item for item in items if item[0] in pairs] for items in order]
    rooms = [sum(2 * counts[i] for _, i in items) for items in order]
    later = [step for step in range(1, len(order)) if inward[step]]
    sent = dict(zip([0], pack(pairs, members, heads, [layout(inward[0])], rooms[:1])))
    sent.update(
        zip(
            later,
            pack(
                pairs, members, heads,
                [layout(inward[step]) for step in later], [rooms[step] for step in later],
            ),
        )
    )
    bias, classes = mask_operands(
        frame_blocks, tile_lists, z, bands, queries.shape[1] * bands, queries.shape[2]
    )
    for step, items in enumerate(order):
        packed, slot, parts = sent.get(step), 2 * len(layout(inward[step])), []
        for name, i in items[len(inward[step]) :]:
            if name == "o":
                while len(owed) <= i:
                    ours = packed is not None and len(owed) == i
                    work_on(len(owed), (packed, slot) if ours else None)
                if packed is None:
                    parts.append(made["o", i])
                else:
                    packed = made["o", i]
            else:
                parts.append(returned(i))
            slot += 2 * counts[i]
        if packed is not None:
            parts.insert(0, packed)
        buffer = jnp.concatenate(parts, axis=1) if len(parts) > 1 else parts[0]
        if step == 2:
            buffer = after(buffer, (bias, classes))
        if arrived:
            buffer = after(buffer, arrived[-1])
        buffer = lax.all_to_all(buffer, group, split_axis=0, concat_axis=0, tiled=True)
        arrived.append(buffer)
        slot = 0
        for name, i in items:
            place[name, i] = (buffer, slot)
            if name == "kv":
                moved = buffer[:, slot : slot + 2 * counts[i]]
                shifted.append(lax.ppermute(moved, "plane", up))
            slot += 2 * counts[i]
    outputs = []
    for name in ("o", "d"):
        used, places = [], []
        for i, count in enumerate(counts):
            buffer, slot = place[name, i]
            if not any(buffer is other for other in used):
                used.append(buffer)
            index = [buffer is other for other in used].index(True)
            places += [(index, slot + 2 * h) for h in range(count)]
        outputs += unpack(used, places, members, heads)
    return tuple(array.reshape(queries.shape) for array in outputs)


def solution(mesh):
    slabs, bands = mesh.shape["tm"], mesh.shape["band"]
    planes = slabs // 2
    split = Mesh(mesh.devices.reshape(planes, 2, bands), ("plane", "half", "band"))
    rows = P(("plane", "half"), "band", None, None)
    return jax.shard_map(
        functools.partial(on_device, planes, bands),
        mesh=split,
        in_specs=(rows, rows, rows, rows, P(), P()),
        out_specs=(rows, rows, rows, rows),
        check_vma=False,
    )
```

```python
import functools
import math

import jax
import jax.numpy as jnp
from jax import lax
from jax.experimental import pallas as pl
from jax.experimental.pallas import tpu as pltpu
from jax.sharding import Mesh, PartitionSpec as P

HEAD_DIM = 128
TT = 2
TH = 8
TW = 8
NTW = 2
TPS = 4
K_NB = 10
MASKED = -1e30
CHUNKS = (2, 1, 2)
ORDER = (
    (("kv", 0),),
    (("kv", 1), ("qc", 0)),
    (("kv", 2), ("qc", 1)),
    (("qc", 2), ("o", 0)),
    (("o", 1), ("d", 0)),
    (("o", 2), ("d", 1)),
    (("d", 2),),
)
VMEM_LIMIT = 32 * 1024 * 1024


STEPS = 2


def hbm(shape, dtype):
    return pltpu.HBM(shape, dtype)


def in_hbm(arrays):
    return [pltpu.with_memory_space_constraint(array, pltpu.HBM) for array in arrays]


def pack(pairs, members, heads, layouts, rooms):
    names = sorted({name for layout in layouts for name, _ in layout})
    arrays = [array for name in names for array in pairs[name]]
    tokens, width = arrays[0].shape
    here = members // STEPS

    def body(*refs):
        ins, outs = refs[: len(arrays)], refs[len(arrays) :]
        for layout, out in zip(layouts, outs):
            for p in range(here):
                for slot, (name, head) in enumerate(layout):
                    start = (p * heads + head) * HEAD_DIM
                    for a in range(2):
                        source = ins[2 * names.index(name) + a]
                        out[p, 2 * slot + a] = source[:, start : start + HEAD_DIM]

    shapes = [(2 * len(layout), tokens, HEAD_DIM) for layout in layouts]
    return pl.pallas_call(
        body,
        grid=(STEPS,),
        out_shape=[
            hbm((members, room, tokens, HEAD_DIM), arrays[0].dtype) for room in rooms
        ],
        in_specs=[pl.BlockSpec((tokens, width // STEPS), lambda i: (0, i))] * len(arrays),
        out_specs=[pl.BlockSpec((here, *shape), lambda i: (i, 0, 0, 0)) for shape in shapes],
        compiler_params=pltpu.CompilerParams(vmem_limit_bytes=VMEM_LIMIT),
        cost_estimate=pl.CostEstimate(
            flops=0, bytes_accessed=4 * sum(array.size for array in arrays), transcendentals=0
        ),
        name="pack",
    )(*in_hbm(arrays))


def unpack(buffers, places, members, heads):
    tokens = buffers[0].shape[2]
    here = members // STEPS

    def body(*refs):
        ins, outs = refs[: len(buffers)], refs[len(buffers) :]
        for p in range(here):
            for head, (buffer, slot) in enumerate(places):
                start = (p * heads + head) * HEAD_DIM
                for a in range(2):
                    outs[a][:, start : start + HEAD_DIM] = ins[buffer][p, slot + a]

    width = members * heads * HEAD_DIM
    return pl.pallas_call(
        body,
        grid=(STEPS,),
        out_shape=[jax.ShapeDtypeStruct((tokens, width), buffers[0].dtype)] * 2,
        in_specs=[
            pl.BlockSpec((here, *buffer.shape[1:]), lambda i: (i, 0, 0, 0)) for buffer in buffers
        ],
        out_specs=[pl.BlockSpec((tokens, width // STEPS), lambda i: (0, i))] * 2,
        compiler_params=pltpu.CompilerParams(vmem_limit_bytes=VMEM_LIMIT),
        cost_estimate=pl.CostEstimate(
            flops=0, bytes_accessed=8 * tokens * width, transcendentals=0
        ),
        name="unpack",
    )(*buffers)


def attention_body(
    bias_ref, class_ref, q_ref, c_ref, kc_ref, vc_ref, kp_ref, vp_ref,
    *refs,
):
    odq_ref, cur_ref, prev_ref, k_all, v_all, dk_all, dv_all = refs[-7:]
    parts, rows = q_ref.shape[0], q_ref.shape[1]
    plane = parts * rows
    slab = plane // 2
    scale = HEAD_DIM ** -0.5
    scale2 = scale * math.log2(math.e)
    half = parts // 2
    k_all[:plane] = kp_ref[...].reshape(plane, HEAD_DIM)
    k_all[plane:] = kc_ref[...].reshape(plane, HEAD_DIM)
    v_all[:plane] = vp_ref[...].reshape(plane, HEAD_DIM)
    v_all[plane:] = vc_ref[...].reshape(plane, HEAD_DIM)
    nt = (((1,), (1,)), ((), ()))
    tn = (((0,), (0,)), ((), ()))
    block = half // 2 * rows
    tile = slab
    tiles = range(3 * slab // tile)
    blocks = [(y, piece) for y in range(2) for piece in range(2)]

    def queries_of(j):
        y, piece = blocks[j]
        here = pl.ds(y * half + piece * (half // 2), half // 2)
        return q_ref[here].reshape(block, HEAD_DIM), c_ref[here].reshape(block, HEAD_DIM)

    def keys_of(j, t):
        start = blocks[j][0] * slab + t * tile
        return slice(start, start + tile)

    def scores(j, t):
        y, piece = blocks[j]
        q, _ = queries_of(j)
        return lax.dot_general(
            jnp.concatenate([q, class_ref[piece * block : (piece + 1) * block]], axis=1),
            jnp.concatenate(
                [k_all[keys_of(j, t)], bias_ref[y, t * tile : (t + 1) * tile]], axis=1
            ),
            nt,
            preferred_element_type=jnp.float32,
        )

    def key_grads(j, t, w, ds):
        q, c = queries_of(j)
        dk = lax.dot_general(ds, q, tn, preferred_element_type=jnp.float32)
        dv = lax.dot_general(w, c, tn, preferred_element_type=jnp.float32)
        keys = keys_of(j, t)
        if j == 0 or (j == 2 and keys.start >= 3 * slab):
            dk_all[keys] = dk
            dv_all[keys] = dv
        else:
            dk_all[keys] += dk
            dv_all[keys] += dv

    ready, top = [], None
    for t in tiles:
        ready.append(scores(0, t))
        top = ready[t] if top is None else jnp.maximum(top, ready[t])
    owed = None
    for j, (y, piece) in enumerate(blocks):
        window = slice(y * slab, (y + 3) * slab)
        here = pl.ds(y * half + piece * (half // 2), half // 2)
        _, c = queries_of(j)
        m = jnp.max(top, axis=1, keepdims=True)
        coming, e, top, total = [], [], None, None
        for t in tiles:
            if j + 1 < len(blocks):
                coming.append(scores(j + 1, t))
                top = coming[t] if top is None else jnp.maximum(top, coming[t])
            e.append(jnp.exp2((ready[t] - m) * scale2))
            total = e[t] if total is None else total + e[t]
        r = 1.0 / jnp.sum(total, axis=1, keepdims=True)
        w = []
        for t in tiles:
            if owed is not None:
                key_grads(j - 1, t, owed[0][t], owed[1][t])
            w.append((e[t] * r).astype(jnp.bfloat16))
        o = jnp.dot(
            jnp.concatenate(w, axis=1), v_all[window], preferred_element_type=jnp.float32
        ).astype(jnp.bfloat16)
        delta = jnp.sum(c.astype(jnp.float32) * o.astype(jnp.float32), axis=1, keepdims=True)
        ds = []
        for t in tiles:
            dp = lax.dot_general(
                c, v_all[keys_of(j, t)], nt, preferred_element_type=jnp.float32
            )
            ds.append((e[t] * r * (dp - delta)).astype(jnp.bfloat16))
        dq = jnp.dot(
            jnp.concatenate(ds, axis=1), k_all[window], preferred_element_type=jnp.float32
        )
        odq_ref[here, 0] = o.reshape(half // 2, rows, HEAD_DIM)
        odq_ref[here, 1] = (dq * scale).astype(jnp.bfloat16).reshape(half // 2, rows, HEAD_DIM)
        ready, owed = coming, (w, ds)
    for t in tiles:
        key_grads(len(blocks) - 1, t, owed[0][t], owed[1][t])
    prev_ref[:, 0] = (dk_all[:plane] * scale).astype(jnp.bfloat16).reshape(kp_ref.shape)
    prev_ref[:, 1] = dv_all[:plane].astype(jnp.bfloat16).reshape(kp_ref.shape)
    cur_ref[:, 0] = (dk_all[plane:] * scale).reshape(kp_ref.shape)
    cur_ref[:, 1] = dv_all[plane:].reshape(kp_ref.shape)


def attention(bias, classes, count, qc, kv, kv_prev, target):
    parts, _, rows, _ = qc[0].shape
    plane = parts * rows
    products = count * 2 * (plane // 2) * 3 * (plane // 2)

    def one(place, a):
        return pl.BlockSpec(
            (parts, None, rows, HEAD_DIM), lambda h: (0, place[1] + 2 * h + a, 0, 0)
        )

    shape = (parts, 2 * count, rows, HEAD_DIM)
    both = pl.BlockSpec((parts, 2, rows, HEAD_DIM), lambda h: (0, h, 0, 0))
    into = both
    if target is not None:
        skip = target[1] // 2
        into = pl.BlockSpec((parts, 2, rows, HEAD_DIM), lambda h: (0, skip + h, 0, 0))
    operands = [(place, a) for place in (qc, kv, kv_prev) for a in range(2)]
    alone = kv[0].shape[1] == 2 * count
    held = [(place, place is qc or (place is kv and not alone)) for place, _ in operands]
    return pl.pallas_call(
        attention_body,
        grid=(count,),
        out_shape=[
            hbm(shape if target is None else target[0].shape, jnp.bfloat16),
            hbm(shape, jnp.float32),
            hbm(shape, jnp.bfloat16),
        ],
        in_specs=[
            pl.BlockSpec(bias.shape, lambda h: (0, 0, 0)),
            pl.BlockSpec(classes.shape, lambda h: (0, 0)),
        ] + [one(place, a) for place, a in operands]
        + ([] if target is None else [pl.BlockSpec(memory_space=pl.ANY)]),
        out_specs=[into, both, both],
        input_output_aliases={} if target is None else {2 + len(operands): 0},
        scratch_shapes=[
            pltpu.VMEM((2 * plane, HEAD_DIM), jnp.bfloat16),
            pltpu.VMEM((2 * plane, HEAD_DIM), jnp.bfloat16),
            pltpu.VMEM((2 * plane, HEAD_DIM), jnp.float32),
            pltpu.VMEM((2 * plane, HEAD_DIM), jnp.float32),
        ],
        compiler_params=pltpu.CompilerParams(vmem_limit_bytes=VMEM_LIMIT),
        cost_estimate=pl.CostEstimate(
            flops=24 * products * HEAD_DIM,
            bytes_accessed=18 * math.prod(shape),
            transcendentals=products,
        ),
        name="attention",
    )(
        *in_hbm([bias, classes]),
        *[in_hbm([place[0]])[0] if pinned else place[0] for place, pinned in held],
        *([] if target is None else [target[0]]),
    )


def mask_operands(frame_blocks, tile_lists, z, bands, frame_rows, frame_cols):
    blocks = frame_blocks.reshape(-1, TT)
    padded = jnp.concatenate([jnp.zeros((2, TT), jnp.int32), blocks])
    tile_rows = frame_rows // TH
    lists = lax.dynamic_slice_in_dim(tile_lists, 2 * z, 2).reshape(2, TPS, K_NB)
    near = lax.dynamic_slice_in_dim(padded, 2 * z, 4)
    key_blocks = jnp.stack([near[0:3], near[1:4]])
    query_blocks = near[2:4]
    distance = 2 - jnp.arange(3, dtype=jnp.int32)
    ids = distance[:, None] * TPS + jnp.arange(TPS, dtype=jnp.int32)[None, :]
    listed = jnp.any(lists[:, :, None, None, :] == ids[None, None, :, :, None], axis=-1)
    present = (2 * z + jnp.arange(2, dtype=jnp.int32))[:, None] >= distance[None, :]
    causal = key_blocks[:, :, :, None] <= query_blocks[:, None, None, :]
    allowed = (
        listed.transpose(0, 2, 3, 1)[:, :, :, None, :, None]
        & present[:, :, None, None, None, None]
        & causal[:, :, None, :, None, :]
    )
    table = jnp.where(allowed, 0.0, MASKED).astype(jnp.bfloat16)
    table = table.reshape(2, 3, tile_rows, NTW, TT, TPS * TT)
    table = table.transpose(0, 1, 2, 4, 3, 5)
    table = jnp.pad(table, [(0, 0)] * 5 + [(0, HEAD_DIM - TPS * TT)])
    per_band = frame_rows // bands
    bias = jnp.broadcast_to(
        table[:, :, :, None, :, None, :, None, :],
        (2, 3, tile_rows, bands // tile_rows, TT, per_band, NTW, TW, HEAD_DIM),
    ).reshape(2, -1, HEAD_DIM)
    row = lax.broadcasted_iota(jnp.int32, (bands * TT * per_band * frame_cols, HEAD_DIM), 0)
    lane = lax.broadcasted_iota(jnp.int32, row.shape, 1)
    per_frame = per_band * frame_cols
    band = row // (TT * per_frame)
    frame = row // per_frame % TT
    tile = band // (bands // tile_rows) * NTW + row % frame_cols // TW
    classes = (lane == tile * TT + frame).astype(jnp.bfloat16)
    return bias, classes


def on_device(planes, bands, queries, key_states, value_states, cotangent, frame_blocks, tile_lists):
    members = 2 * bands
    width = queries.shape[-1]
    heads = width // HEAD_DIM // members
    z = lax.axis_index("plane")
    group = ("half", "band")
    q, k, v, c = (
        array.reshape(-1, width) for array in (queries, key_states, value_states, cotangent)
    )
    up = [(i, i + 1) for i in range(planes - 1)]
    down = [(i + 1, i) for i in range(planes - 1)]

    if sum(CHUNKS) == heads:
        counts, order = CHUNKS, ORDER
    else:
        counts = (heads,)
        order = ((("kv", 0),), (("qc", 0),), (("o", 0),), (("d", 0),))
    firsts = [sum(counts[:i]) for i in range(len(counts))]
    arrived, place, shifted, owed, made, cut = [], {}, [], [], {}, ()

    def after(array, other):
        return lax.optimization_barrier((array, other))[0]

    def layout(items):
        return [(name, firsts[i] + h) for name, i in items for h in range(counts[i])]

    def work_on(i, target):
        odq, dkv, dkv_prev = attention(
            bias, classes, counts[i], place["qc", i], place["kv", i], (shifted[i], 0), target
        )
        made["o", i] = odq
        owed.append((dkv, lax.ppermute(dkv_prev, "plane", down)))

    def returned(i):
        dkv, dkv_next = owed[i]
        if i + 1 < len(owed):
            dkv_next = after(dkv_next, owed[-1][0])
        return (dkv + dkv_next.astype(jnp.float32)).astype(jnp.bfloat16)

    pairs = {"kv": (k, v), "qc": (q, c)}
    inward = [[item for item in items if item[0] in pairs] for items in order]
    rooms = [sum(2 * counts[i] for _, i in items) for items in order]
    later = [step for step in range(1, len(order)) if inward[step]]
    sent = dict(zip([0], pack(pairs, members, heads, [layout(inward[0])], rooms[:1])))
    sent.update(
        zip(
            later,
            pack(
                pairs, members, heads,
                [layout(inward[step]) for step in later], [rooms[step] for step in later],
            ),
        )
    )
    bias, classes = mask_operands(
        frame_blocks, tile_lists, z, bands, queries.shape[1] * bands, queries.shape[2]
    )
    for step, items in enumerate(order):
        packed, slot, parts = sent.get(step), 2 * len(layout(inward[step])), []
        for name, i in items[len(inward[step]) :]:
            if name == "o":
                while len(owed) <= i:
                    ours = packed is not None and len(owed) == i
                    work_on(len(owed), (packed, slot) if ours else None)
                if packed is None:
                    parts.append(made["o", i])
                else:
                    packed = made["o", i]
            else:
                parts.append(returned(i))
            slot += 2 * counts[i]
        if packed is not None:
            parts.insert(0, packed)
        buffer = jnp.concatenate(parts, axis=1) if len(parts) > 1 else parts[0]
        if step == 2:
            buffer = after(buffer, (bias, classes, cut))
        if arrived:
            buffer = after(buffer, arrived[-1])
        buffer = lax.all_to_all(buffer, group, split_axis=0, concat_axis=0, tiled=True)
        arrived.append(buffer)
        slot = 0
        for name, i in items:
            place[name, i] = (buffer, slot)
            if name == "kv":
                cut = buffer[:, slot : slot + 2 * counts[i]]
                shifted.append(lax.ppermute(cut, "plane", up))
            slot += 2 * counts[i]
    outputs = []
    for name in ("o", "d"):
        used, places = [], []
        for i, count in enumerate(counts):
            buffer, slot = place[name, i]
            if not any(buffer is other for other in used):
                used.append(buffer)
            index = [buffer is other for other in used].index(True)
            places += [(index, slot + 2 * h) for h in range(count)]
        outputs += unpack(used, places, members, heads)
    return tuple(array.reshape(queries.shape) for array in outputs)


def solution(mesh):
    slabs, bands = mesh.shape["tm"], mesh.shape["band"]
    planes = slabs // 2
    split = Mesh(mesh.devices.reshape(planes, 2, bands), ("plane", "half", "band"))
    rows = P(("plane", "half"), "band", None, None)
    return jax.shard_map(
        functools.partial(on_device, planes, bands),
        mesh=split,
        in_specs=(rows, rows, rows, rows, P(), P()),
        out_specs=(rows, rows, rows, rows),
        check_vma=False,
    )
```
